32 devices in a mesh: tm: 2 (over x), space: 16 (over z, y, core).
Axes of the slice: x: 2, y: 2, z: 4, core: 2. Of those that a mesh axis runs over, the one named last changes fastest.
Arguments:
- orbitals: bfloat16 [13824, 320], P('space'), may hold values from -6 to 6
- gaps: float32 [320], replicated, may hold values from 0.005 to 50
- times: float32 [2], P('tm'), may hold values from 0.01 to 100, as said below
- cos_weights: float32 [2, 2], replicated, may hold values from -1 to 1
Outputs:
- polarizability: float32 [2, 864, 864], P('tm', 'space')
The draws below stay inside these ranges and needn't reach their ends.
Inputs may be any that keep to these rules, and one draw needn't show every extreme that they name: times rise with their index.
All inputs are finite; a program needn't handle non-finite values.
Results may differ from the reference program's by a relative error of at most 0.0044.
Values may be sent and summed in bfloat16 or wider, within the bound.
No kernel may reach another device: no remote copies, remote signals or barrier semaphores. Data moves between devices by JAX's collectives and lax.ppermute only.
A program may use at most 192 MiB of HBM per device.

```python
import math
import jax
import jax.numpy as jnp
from jax import lax

SIDE = 24
NG = 864
NOCC = 64
NEMP = 256
R = 13824
NORB = 320
NT = 2
NW = 2


def draw_gaps(key, part):
    level = jax.random.uniform(key, (NORB,), jnp.float32, 0.0, 1.0)
    return 0.005 * jnp.exp(level * level * math.log(10000.0))


def draw_times(key, part):
    position = jnp.arange(NT, dtype=jnp.float32)
    jitter = jax.random.uniform(key, (NT,), jnp.float32, 0.3, 0.7)
    return 0.01 * jnp.exp((position + jitter) / NT * math.log(10000.0))


def draw_cos_weights(key, part):
    phase_key, size_key = jax.random.split(jax.random.fold_in(key, 17))
    frequency = jnp.arange(NW, dtype=jnp.float32)[:, None]
    moment_index = jnp.arange(NT, dtype=jnp.float32)[None, :]
    phase = jax.random.uniform(phase_key, (NW, 1), jnp.float32, -math.pi, math.pi)
    amplitude = jax.random.uniform(size_key, (NW, NT), jnp.float32, 0.5, 1.0)
    ramp = 0.5 + 0.5 * (moment_index + 1.0) / NT
    angle = math.pi * (frequency + 0.5) * (moment_index + 0.5) / NT + phase
    return amplitude * ramp * jnp.cos(angle)


def steps_of(own_key, dims, cuts, smallest, top_value):
    level = 1.0
    for dim, blocks in cuts:
        draws = jax.random.uniform(jax.random.fold_in(jax.random.fold_in(own_key, 6), dim), (blocks,), jnp.float32, smallest / len(cuts), top_value / len(cuts))
        level = level * jnp.repeat(jnp.exp(draws), dims[dim] // blocks).reshape((-1,) + (1,) * (len(dims) - 1 - dim))
    return level


def noise(rng, shape, width, reach, cuts=(), kind=jnp.bfloat16):
    loudness = steps_of(rng, shape, cuts, -0.22, 0.18) if cuts else 1.0
    result = jax.random.normal(rng, shape, jnp.float32) * width * loudness
    return jnp.minimum(jnp.maximum(result, -reach), reach).astype(kind)


def setup_inputs(seed: int = 0) -> dict:
    splits = jax.random.split(jax.random.key(seed), 5)
    orbitals = noise(splits[0], (R, NORB), 1.0, 6.0, ((0, 16),))
    gaps = draw_gaps(jax.random.fold_in(splits[4], 71), 0)
    times = draw_times(jax.random.fold_in(splits[4], 71), 0)
    cos_weights = draw_cos_weights(jax.random.fold_in(splits[4], 71), 0)
    return dict(orbitals=orbitals, gaps=gaps, times=times, cos_weights=cos_weights)


def plane_table(grid_side, mode_count):
    side_index = jnp.arange(grid_side, dtype=jnp.int32)
    wave_index = jnp.arange(mode_count // 2, dtype=jnp.int32)
    span_first = grid_side // 2
    span_second = grid_side // 4
    wave_first = wave_index % span_first - span_first // 2
    wave_second = wave_index // span_first % span_second - span_second // 2
    wave_third = wave_index // (span_first * span_second) + 1

    def factor(wave_vector):
        step_counts = jnp.mod(wave_vector[:, None] * side_index[None, :], grid_side)
        angles = step_counts.astype(jnp.float32) * (2.0 * math.pi / grid_side)
        return (jnp.cos(angles), jnp.sin(angles))
    cos_first, sin_first = factor(wave_first)
    cos_second, sin_second = factor(wave_second)
    cos_third, sin_third = factor(wave_third)
    cos_first = cos_first[:, :, None, None]
    sin_first = sin_first[:, :, None, None]
    cos_second = cos_second[:, None, :, None]
    sin_second = sin_second[:, None, :, None]
    cos_third = cos_third[:, None, None, :]
    sin_third = sin_third[:, None, None, :]
    inner_cos = cos_second * cos_third - sin_second * sin_third
    inner_sin = sin_second * cos_third + cos_second * sin_third
    cos_whole = cos_first * inner_cos - sin_first * inner_sin
    sin_whole = sin_first * inner_cos + cos_first * inner_sin
    half_count = mode_count // 2
    scaling = math.sqrt(2.0 / grid_side ** 3)
    joined = jnp.concatenate([cos_whole.reshape(half_count, -1), sin_whole.reshape(half_count, -1)], axis=0)
    return (joined * scaling).astype(jnp.bfloat16)

def reference(orbitals, gaps, times, cos_weights):
    block = SIDE * SIDE
    blocks = R // block
    column_scale = jnp.concatenate([jnp.full((NOCC,), NOCC ** (-0.5), jnp.float32), jnp.full((NEMP,), NEMP ** (-0.5), jnp.float32)])
    table = plane_table(SIDE, NG)

    def one_time(tau_value):
        factors = jnp.exp(-gaps * tau_value) * column_scale
        weighted = (orbitals.astype(jnp.float32) * factors[None, :]).astype(jnp.bfloat16)

        def first_pass(carry, block_index):
            row_start = (block_index * block).astype(jnp.int32)
            row_block = lax.dynamic_slice_in_dim(orbitals, row_start, block, 0)
            green_occ = jnp.dot(row_block[:, :NOCC], weighted[:, :NOCC].T, preferred_element_type=jnp.float32)
            green_emp = jnp.dot(row_block[:, NOCC:], weighted[:, NOCC:].T, preferred_element_type=jnp.float32)
            chi_block = (green_occ * green_emp).astype(jnp.bfloat16)
            table_block = lax.dynamic_slice_in_dim(table, row_start, block, 1)
            return (carry + jnp.dot(table_block, chi_block, preferred_element_type=jnp.float32), None)
        half, _ = lax.scan(first_pass, jnp.zeros((NG, R), jnp.float32), jnp.arange(blocks, dtype=jnp.int32))
        half = half.astype(jnp.bfloat16)
        return jnp.dot(half, table.T, preferred_element_type=jnp.float32)
    moments = lax.map(one_time, times)
    return jnp.einsum('wt,tgh->wgh', cos_weights, moments, precision=lax.Precision.HIGHEST)
```

```python
import functools
import math

import jax
import jax.numpy as jnp
from jax import lax
from jax.experimental import pallas as pl
from jax.experimental.pallas import tpu as pltpu
from jax.sharding import PartitionSpec as P

SIDE = 24
NG = 864
NOCC = 64
NEMP = 256
LANES = 128


def round_up(value, step):
    return -(-value // step) * step


def class_waves(mode_count, grid_side):
    first, second = grid_side // 2, grid_side // 4
    third = mode_count // 2 // (first * second)
    column = jnp.arange(mode_count // 4, dtype=jnp.int32)
    a_step = column % (first // 2)
    b_step = column // (first // 2) % (second // 2)
    c_step = column // (first // 2 * (second // 2)) % third
    sine = column // (first // 2 * (second // 2) * third)
    classes = []
    for a_odd in range(2):
        for b_odd in range(2):
            a_index = 2 * a_step + (a_odd + first // 2) % 2
            b_index = 2 * b_step + (b_odd + second // 2) % 2
            row = sine * (mode_count // 2) + c_step * first * second + b_index * first + a_index
            classes.append((a_index - first // 2, b_index - second // 2, c_step + 1, sine, row))
    return classes


def class_tables(grid_side, mode_count, steps, depth_pad, width_pad):
    half = grid_side // 2
    x = jnp.arange(half, dtype=jnp.int32)
    y = jnp.arange(half, dtype=jnp.int32)
    z = jnp.arange(grid_side, dtype=jnp.int32)
    yz_y = jnp.repeat(y, grid_side)
    yz_z = jnp.tile(z, half)
    unit = 2.0 * math.pi / grid_side
    scaling = math.sqrt(2.0 / grid_side**3)
    tables = []
    for a, b, c, sine, _ in class_waves(mode_count, grid_side):
        p = jnp.mod(x[:, None] * a[None, :], grid_side).astype(jnp.float32) * unit
        q = jnp.mod(yz_y[:, None] * b[None, :] + yz_z[:, None] * c[None, :], grid_side).astype(jnp.float32) * unit
        cos_p, sin_p = jnp.cos(p), jnp.sin(p)
        cos_q, sin_q = jnp.cos(q), jnp.sin(q)
        is_sine = (sine == 1)[None, :]
        first = jnp.where(is_sine, sin_q, cos_q) * scaling
        second = jnp.where(is_sine, cos_q, -sin_q) * scaling
        table = cos_p[:, None, :] * first[None] + sin_p[:, None, :] * second[None]
        tables.append(table.astype(jnp.bfloat16).reshape(steps, -1, table.shape[-1]))
    stacked = jnp.stack(tables, axis=1)
    return jnp.pad(
        stacked,
        ((0, 0), (0, 0), (0, depth_pad - stacked.shape[2]), (0, width_pad - stacked.shape[3])),
    )


def column_order(grid_side, mode_count, width_pad):
    rows = jnp.concatenate(
        [
            jnp.pad(wave[4], (0, width_pad - mode_count // 4), constant_values=-1)
            for wave in class_waves(mode_count, grid_side)
        ]
    )
    return (rows[:, None] == jnp.arange(mode_count, dtype=jnp.int32)[None, :]).astype(jnp.bfloat16)


def pair_kernel(
    occ_ref, emp_ref, table_ref, weight_ref, order_ref, out_ref, occ_wide, emp_wide, product, rho
):
    step = pl.program_id(0)
    shards, n_occ, n_rows = occ_ref.shape[1:]
    n_emp = emp_ref.shape[2]
    depth = product.shape[2]
    joined = max(1, 16 // n_emp)
    plane = n_rows * shards // (3 * 2)

    def halves(ref):
        parts = []
        for far in range(2):
            rows = [ref[far, shard].astype(jnp.float32) for shard in range(shards)]
            for upper in range(2):
                pieces = []
                for x in range(3):
                    start = (2 * x + upper) * plane
                    stop = start + plane
                    while start < stop:
                        shard, offset = divmod(start, n_rows)
                        count = min(stop - start, n_rows - offset)
                        pieces.append(rows[shard][:, offset : offset + count])
                        start += count
                pieces.append(jnp.zeros((ref.shape[2], depth - 3 * plane), jnp.float32))
                parts.append(jnp.concatenate(pieces, axis=1))
        return parts

    for index, part in enumerate(halves(occ_ref)):
        occ_wide[index] = part
    for index, part in enumerate(halves(emp_ref)):
        emp_wide[index] = part

    def eight_occupied(group, carry):
        base = pl.multiple_of(group * 8, 8)
        for lane in range(0, depth, LANES):
            cut = slice(lane, lane + LANES)
            occ_rows = [occ_wide[k, pl.ds(base, 8), cut] for k in range(4)]
            emp_rows = [emp_wide[k, :, cut] for k in range(4)]
            for first in range(0, 8, joined):
                values = [[], [], [], []]
                for i in range(first, first + joined):
                    near_low, near_high, far_low, far_high = (
                        occ_rows[k][i : i + 1] * emp_rows[k] for k in range(4)
                    )
                    even_low, odd_low = near_low + far_low, near_low - far_low
                    even_high, odd_high = near_high + far_high, near_high - far_high
                    values[0].append(even_low + even_high)
                    values[1].append(even_low - even_high)
                    values[2].append(odd_low + odd_high)
                    values[3].append(odd_low - odd_high)
                start = pl.multiple_of((base + first) * n_emp, joined * n_emp)
                for k in range(4):
                    value = jnp.concatenate(values[k], axis=0) if joined > 1 else values[k][0]
                    product[k, pl.ds(start, joined * n_emp), cut] = value.astype(jnp.bfloat16)
        return carry

    lax.fori_loop(0, n_occ // 8, eight_occupied, 0)

    for k in range(4):
        term = jnp.dot(product[k], table_ref[0, k], preferred_element_type=jnp.float32)

        @pl.when(step == 0)
        def _():
            rho[k] = term

        @pl.when(step > 0)
        def _():
            rho[k] += term

    @pl.when(step == pl.num_programs(0) - 1)
    def _():
        columns = jnp.concatenate([rho[k].astype(jnp.bfloat16) for k in range(4)], axis=1)
        ordered = jnp.dot(columns, order_ref[...], preferred_element_type=jnp.float32)
        weighted = (ordered * weight_ref[...]).astype(jnp.bfloat16)
        moment = lax.dot_general(
            weighted,
            ordered.astype(jnp.bfloat16),
            (((0,), (0,)), ((), ())),
            preferred_element_type=jnp.float32,
        )
        block = out_ref.shape[1]
        for k in range(out_ref.shape[0]):
            out_ref[k] = moment[k * block : (k + 1) * block].astype(jnp.bfloat16)


def pair_moment(occ, emp, tables, weights, order, blocks):
    shards, n_occ, n_rows = occ.shape
    n_emp = emp.shape[1]
    steps, _, depth, width = tables.shape
    group = shards // (2 * steps)
    pairs = n_occ * n_emp
    modes = order.shape[1]
    return pl.pallas_call(
        pair_kernel,
        grid=(steps,),
        out_shape=jax.ShapeDtypeStruct((blocks, modes // blocks, modes), jnp.bfloat16),
        in_specs=[
            pl.BlockSpec((2, group, n_occ, n_rows), lambda s: (0, s, 0, 0)),
            pl.BlockSpec((2, group, n_emp, n_rows), lambda s: (0, s, 0, 0)),
            pl.BlockSpec((1, 4, depth, width), lambda s: (s, 0, 0, 0)),
            pl.BlockSpec((pairs, 1), lambda s: (0, 0)),
            pl.BlockSpec((4 * width, modes), lambda s: (0, 0)),
        ],
        out_specs=pl.BlockSpec((blocks, modes // blocks, modes), lambda s: (0, 0, 0)),
        scratch_shapes=[
            pltpu.VMEM((4, n_occ, depth), jnp.float32),
            pltpu.VMEM((4, n_emp, depth), jnp.float32),
            pltpu.VMEM((4, pairs, depth), jnp.bfloat16),
            pltpu.VMEM((4, pairs, width), jnp.float32),
        ],
        compiler_params=pltpu.CompilerParams(vmem_limit_bytes=56 * 1024 * 1024),
        cost_estimate=pl.CostEstimate(
            flops=2 * steps * 4 * pairs * depth * width, bytes_accessed=12 * 2**20, transcendentals=0
        ),
        name="pair_moment",
    )(
        occ.reshape(2, shards // 2, n_occ, n_rows),
        emp.reshape(2, shards // 2, n_emp, n_rows),
        tables,
        weights,
        order,
    )


def local(space, tm, orbitals, gaps, times, cos_weights):
    rows = orbitals.shape[0]
    columns = orbitals.T
    own_emp = NEMP // space
    occ = lax.all_gather(columns[:NOCC], "space", axis=0)
    emp = lax.all_to_all(
        columns[NOCC:].reshape(space, own_emp, rows), "space", split_axis=0, concat_axis=0
    )

    planes = 3
    steps = SIDE // 2 // planes
    depth = round_up(planes * SIDE * SIDE // 2, LANES)
    width = round_up(NG // 4, 2 * LANES)
    tables = class_tables(SIDE, NG, steps, depth, width)
    order = column_order(SIDE, NG, width)

    every_time = lax.all_gather(times, "tm", axis=0, tiled=True)
    factors = jnp.exp(-gaps[None, :] * every_time[:, None])
    occ_factors = factors[:, :NOCC] * NOCC ** (-0.5)
    emp_factors = lax.dynamic_slice_in_dim(
        factors[:, NOCC:], lax.axis_index("space") * own_emp, own_emp, 1
    ) * NEMP ** (-0.5)
    own_count = cos_weights.shape[0] // tm
    own_weights = lax.dynamic_slice_in_dim(
        cos_weights, lax.axis_index("tm") * own_count, own_count, 0
    )
    pair_weights = jnp.sum(
        own_weights[:, :, None, None] * (occ_factors[:, :, None] * emp_factors[:, None, :])[None], axis=1
    ).reshape(own_count, NOCC * own_emp, 1)

    results = []
    for w in range(own_count):
        partial = pair_moment(occ, emp, tables, pair_weights[w], order, space)
        parts = lax.all_to_all(partial, "space", split_axis=0, concat_axis=0)
        results.append(jnp.sum(parts.astype(jnp.float32), axis=0))
    return jnp.stack(results)


def solution(mesh):
    return jax.shard_map(
        functools.partial(local, mesh.shape["space"], mesh.shape["tm"]),
        mesh=mesh,
        in_specs=(P("space", None), P(), P("tm"), P()),
        out_specs=P("tm", "space", None),
        check_vma=False,
    )
```

```python
import functools
import math

import jax
import jax.numpy as jnp
from jax import lax
from jax.experimental import pallas as pl
from jax.experimental.pallas import tpu as pltpu
from jax.sharding import PartitionSpec as P

SIDE = 24
NG = 864
NOCC = 64
NEMP = 256
LANES = 128


def round_up(value, step):
    return -(-value // step) * step


def class_waves(mode_count, grid_side):
    first, second = grid_side // 2, grid_side // 4
    third = mode_count // 2 // (first * second)
    column = jnp.arange(mode_count // 4, dtype=jnp.int32)
    a_step = column % (first // 2)
    b_step = column // (first // 2) % (second // 2)
    c_step = column // (first // 2 * (second // 2)) % third
    sine = column // (first // 2 * (second // 2) * third)
    classes = []
    for a_odd in range(2):
        for b_odd in range(2):
            a_index = 2 * a_step + (a_odd + first // 2) % 2
            b_index = 2 * b_step + (b_odd + second // 2) % 2
            row = sine * (mode_count // 2) + c_step * first * second + b_index * first + a_index
            classes.append((a_index - first // 2, b_index - second // 2, c_step + 1, sine, row))
    return classes


def class_tables(grid_side, mode_count, steps, depth_pad, width_pad):
    half = grid_side // 2
    x = jnp.arange(half, dtype=jnp.int32)
    y = jnp.arange(half, dtype=jnp.int32)
    z = jnp.arange(grid_side, dtype=jnp.int32)
    yz_y = jnp.repeat(y, grid_side)
    yz_z = jnp.tile(z, half)
    unit = 2.0 * math.pi / grid_side
    scaling = math.sqrt(2.0 / grid_side**3)
    tables = []
    for a, b, c, sine, _ in class_waves(mode_count, grid_side):
        p = jnp.mod(x[:, None] * a[None, :], grid_side).astype(jnp.float32) * unit
        q = jnp.mod(yz_y[:, None] * b[None, :] + yz_z[:, None] * c[None, :], grid_side).astype(jnp.float32) * unit
        cos_p, sin_p = jnp.cos(p), jnp.sin(p)
        cos_q, sin_q = jnp.cos(q), jnp.sin(q)
        is_sine = (sine == 1)[None, :]
        first = jnp.where(is_sine, sin_q, cos_q) * scaling
        second = jnp.where(is_sine, cos_q, -sin_q) * scaling
        table = cos_p[:, None, :] * first[None] + sin_p[:, None, :] * second[None]
        tables.append(table.astype(jnp.bfloat16).reshape(steps, -1, table.shape[-1]))
    stacked = jnp.stack(tables, axis=1)
    return jnp.pad(
        stacked,
        ((0, 0), (0, 0), (0, depth_pad - stacked.shape[2]), (0, width_pad - stacked.shape[3])),
    )


def column_order(grid_side, mode_count, width_pad):
    rows = jnp.concatenate(
        [
            jnp.pad(wave[4], (0, width_pad - mode_count // 4), constant_values=-1)
            for wave in class_waves(mode_count, grid_side)
        ]
    )
    return (rows[:, None] == jnp.arange(mode_count, dtype=jnp.int32)[None, :]).astype(jnp.bfloat16)


def reversed_bits(value, bits):
    return sum(((value >> k) & 1) << (bits - 1 - k) for k in range(bits))


def pair_kernel(
    place_ref,
    weight_ref,
    emp_own_ref,
    emp_other_ref,
    table_hbm,
    order_hbm,
    *refs,
):
    chips = emp_own_ref.shape[0]
    occ_refs = refs[:chips]
    keep_ref, send_ref = refs[chips : chips + 2]
    raw_occ, raw_emp, occ_wide, emp_wide, first, second, rho, blocks, table, order, table_sem, order_sem = refs[
        chips + 2 :
    ]
    steps, _, depth, width = table.shape
    n_occ, n_rows = raw_occ.shape[1:]
    n_emp = raw_emp.shape[1]
    per_group = 2 * chips // (2 * steps)
    plane = SIDE * SIDE // 2

    table_copies = [
        pltpu.make_async_copy(table_hbm.at[s], table.at[s], table_sem.at[s]) for s in range(steps)
    ]
    for copy in table_copies:
        copy.start()
    order_copy = pltpu.make_async_copy(order_hbm, order, order_sem)
    order_copy.start()

    core = place_ref[chips]
    me = place_ref[chips + 1]
    for index, ref in enumerate(occ_refs):
        chip = place_ref[index]
        raw_occ[chip * 2 + core] = ref[0]
        raw_occ[chip * 2 + 1 - core] = ref[1]
    for chip in range(chips):
        raw_emp[chip * 2 + core] = emp_own_ref[chip]
        raw_emp[chip * 2 + 1 - core] = emp_other_ref[chip]

    def halves(raw, group, upper):
        pieces = []
        for x in range(3):
            start = (2 * x + upper) * plane
            stop = start + plane
            while start < stop:
                shard, offset = divmod(start, n_rows)
                count = min(stop - start, n_rows - offset)
                rows = raw[group * per_group + shard].astype(jnp.float32)
                pieces.append(rows[:, offset : offset + count])
                start += count
        pieces.append(jnp.zeros((raw.shape[1], depth - 3 * plane), jnp.float32))
        return jnp.concatenate(pieces, axis=1)

    for group in range(2 * steps):
        for upper in range(2):
            occ_wide[group, upper] = halves(raw_occ, group, upper)
            emp_wide[group, upper] = halves(raw_emp, group, upper).astype(jnp.bfloat16)

    rho[...] = jnp.zeros_like(rho)
    quarter = n_occ // 4

    def build(step, target, part):
        sources = [(step, 0), (step, 1), (step + steps, 0), (step + steps, 1)]
        for lane in range(0, depth, LANES):
            cut = slice(lane, lane + LANES)
            occ_rows = [
                occ_wide[group, upper, part * quarter : (part + 1) * quarter, cut] for group, upper in sources
            ]
            emp_rows = [emp_wide[group, upper, :, cut] for group, upper in sources]
            for i in range(quarter):
                near_low, near_high, far_low, far_high = (
                    jnp.broadcast_to(occ_rows[k][i : i + 1], (n_emp, LANES)).astype(jnp.bfloat16) * emp_rows[k]
                    for k in range(4)
                )
                even_low, odd_low = near_low + far_low, near_low - far_low
                even_high, odd_high = near_high + far_high, near_high - far_high
                start = (part * quarter + i) * n_emp
                target[0, start : start + n_emp, cut] = even_low + even_high
                target[1, start : start + n_emp, cut] = even_low - even_high
                target[2, start : start + n_emp, cut] = odd_low + odd_high
                target[3, start : start + n_emp, cut] = odd_low - odd_high

    def multiply(step, source, k):
        rho[k] += jnp.dot(source[k], table[step, k], preferred_element_type=jnp.float32)

    for part in range(4):
        build(0, first, part)

    def two_steps(t, carry):
        for offset, (now, later) in enumerate(((first, second), (second, first))):
            step = 2 * t + offset
            pltpu.make_async_copy(table_hbm.at[step], table.at[step], table_sem.at[step]).wait()
            following = lax.rem(step + 1, steps)
            for k in range(4):
                build(following, later, k)
                multiply(step, now, k)
        return carry

    lax.fori_loop(0, steps // 2, two_steps, 0)

    order_copy.wait()
    columns = jnp.concatenate([rho[k].astype(jnp.bfloat16) for k in range(4)], axis=1)
    ordered = jnp.dot(columns, order[...], preferred_element_type=jnp.float32)
    weighted = (ordered * weight_ref[...]).astype(jnp.bfloat16)
    moment = lax.dot_general(
        weighted,
        ordered.astype(jnp.bfloat16),
        (((0,), (0,)), ((), ())),
        preferred_element_type=jnp.float32,
    )
    count, rows = blocks.shape[:2]
    bits = count.bit_length() - 1
    for k in range(count):
        blocks[k] = moment[k * rows : (k + 1) * rows]
    for k in range(count // 2):
        keep_ref[k] = blocks[jnp.bitwise_xor(me, reversed_bits(k, bits))]
        send_ref[k] = blocks[jnp.bitwise_xor(me, reversed_bits(k + count // 2, bits))].astype(jnp.bfloat16)


def pair_moment(place, weights, occ_blocks, emp_own, emp_other, tables, order):
    chips, n_emp, n_rows = emp_own.shape
    n_occ = occ_blocks[0].shape[1]
    steps, _, depth, width = tables.shape
    pairs = n_occ * n_emp
    modes = order.shape[1]
    blocks = 2 * chips
    rows = modes // blocks
    vmem = pl.BlockSpec(memory_space=pltpu.VMEM)
    hbm = pl.BlockSpec(memory_space=pl.ANY)
    return pl.pallas_call(
        pair_kernel,
        out_shape=(
            jax.ShapeDtypeStruct((blocks // 2, rows, modes), jnp.float32),
            jax.ShapeDtypeStruct((blocks // 2, rows, modes), jnp.bfloat16),
        ),
        in_specs=[pl.BlockSpec(memory_space=pltpu.SMEM), vmem, vmem, vmem, hbm, hbm] + [vmem] * chips,
        out_specs=(vmem, vmem),
        scratch_shapes=[
            pltpu.VMEM((2 * chips, n_occ, n_rows), jnp.bfloat16),
            pltpu.VMEM((2 * chips, n_emp, n_rows), jnp.bfloat16),
            pltpu.VMEM((2 * steps, 2, n_occ, depth), jnp.float32),
            pltpu.VMEM((2 * steps, 2, n_emp, depth), jnp.bfloat16),
            pltpu.VMEM((4, pairs, depth), jnp.bfloat16),
            pltpu.VMEM((4, pairs, depth), jnp.bfloat16),
            pltpu.VMEM((4, pairs, width), jnp.float32),
            pltpu.VMEM((blocks, rows, modes), jnp.float32),
            pltpu.VMEM(tables.shape, jnp.bfloat16),
            pltpu.VMEM(order.shape, jnp.bfloat16),
            pltpu.SemaphoreType.DMA((steps,)),
            pltpu.SemaphoreType.DMA,
        ],
        compiler_params=pltpu.CompilerParams(vmem_limit_bytes=60 * 1024 * 1024),
        cost_estimate=pl.CostEstimate(
            flops=2 * steps * 4 * pairs * depth * width, bytes_accessed=16 * 2**20, transcendentals=0
        ),
        name="pair_moment",
    )(place, weights, emp_own, emp_other, tables, order, *occ_blocks)


def ring_of(chips):
    return list(range(0, chips, 2)) + list(range(chips - 1, 0, -2))


def gather_ring(block, chips):
    ring = ring_of(chips)
    ahead, back = [], []
    for position in range(chips):
        for core in range(2):
            here = 2 * ring[position] + core
            right = 2 * ring[(position + 1) % chips] + core
            ahead.append((here, right))
            back.append((right, here))
    found = [block]
    offsets = [0]
    from_left = from_right = block
    for hop in range(1, chips // 2 + 1):
        from_left = lax.ppermute(from_left, "space", ahead)
        found.append(from_left)
        offsets.append(-hop)
        if 2 * hop < chips:
            from_right = lax.ppermute(from_right, "space", back)
            found.append(from_right)
            offsets.append(hop)
    return found, offsets


def local(space, tm, orbitals, gaps, times, cos_weights):
    rows = orbitals.shape[0]
    chips = space // 2
    columns = orbitals.T
    own_occ, own_emp = NOCC // 2, NEMP // chips
    me = lax.axis_index("space")
    core, chip = me % 2, me // 2
    swap = [(d, d ^ 1) for d in range(space)]

    occ = columns[:NOCC].reshape(2, own_occ, rows)
    occ_mine = lax.dynamic_index_in_dim(occ, core, 0, keepdims=False)
    occ_theirs = lax.dynamic_index_in_dim(occ, 1 - core, 0, keepdims=False)
    occ_pair = jnp.stack([occ_mine, lax.ppermute(occ_theirs, "space", swap)])
    emp_own = lax.all_to_all(
        columns[NOCC:].reshape(chips, own_emp, rows),
        "space",
        split_axis=0,
        concat_axis=0,
        axis_index_groups=[[2 * k + c for k in range(chips)] for c in range(2)],
    )
    occ_blocks, offsets = gather_ring(occ_pair, chips)
    emp_other = lax.ppermute(emp_own, "space", swap)

    ring = jnp.array(ring_of(chips), jnp.int32)
    position = jnp.argmax(ring == chip)
    place = jnp.concatenate(
        [ring[(position + jnp.array(offsets, jnp.int32)) % chips], jnp.stack([core, me])]
    ).astype(jnp.int32)

    planes = 3
    steps = SIDE // 2 // planes
    depth = round_up(planes * SIDE * SIDE // 2, LANES)
    width = round_up(NG // 4, 2 * LANES)
    tables = class_tables(SIDE, NG, steps, depth, width)
    order = column_order(SIDE, NG, width)

    own_count = cos_weights.shape[0] // tm
    tm_index = lax.axis_index("tm")
    pair_weights = 0.0
    for hop in range(tm):
        source = (tm_index + hop) % tm
        their_times = times
        if hop:
            their_times = lax.ppermute(times, "tm", [((d + hop) % tm, d) for d in range(tm)])
        factors = jnp.exp(-gaps[None, :] * their_times[:, None])
        occ_factors = lax.dynamic_slice_in_dim(factors, core * own_occ, own_occ, 1) * NOCC ** (-0.5)
        emp_factors = lax.dynamic_slice_in_dim(factors, NOCC + chip * own_emp, own_emp, 1) * NEMP ** (-0.5)
        weights = lax.dynamic_slice(
            cos_weights,
            (tm_index * own_count, source * times.shape[0]),
            (own_count, times.shape[0]),
        )
        pair_weights = pair_weights + jnp.sum(
            weights[:, :, None, None] * (occ_factors[:, :, None] * emp_factors[:, None, :])[None], axis=1
        )
    pair_weights = pair_weights.reshape(own_count, own_occ * own_emp, 1)

    results = []
    for w in range(own_count):
        keep, send = pair_moment(place, pair_weights[w], occ_blocks, emp_own, emp_other, tables, order)
        distance = 1
        while True:
            received = lax.ppermute(send, "space", [(d, d ^ distance) for d in range(space)])
            total = keep + received.astype(jnp.float32)
            if total.shape[0] == 1:
                break
            half = total.shape[0] // 2
            keep, send = total[:half], total[half:].astype(jnp.bfloat16)
            distance *= 2
        results.append(total[0])
    return jnp.stack(results)


def solution(mesh):
    return jax.shard_map(
        functools.partial(local, mesh.shape["space"], mesh.shape["tm"]),
        mesh=mesh,
        in_specs=(P("space", None), P(), P("tm"), P()),
        out_specs=P("tm", "space", None),
        check_vma=False,
    )
```

```python
import functools
import math

import jax
import jax.numpy as jnp
from jax import lax
from jax.experimental import pallas as pl
from jax.experimental.pallas import tpu as pltpu
from jax.sharding import PartitionSpec as P

SIDE = 24
NG = 864
NOCC = 64
NEMP = 256
LANES = 128


def round_up(value, step):
    return -(-value // step) * step


def class_waves(mode_count, grid_side, width):
    first, second = grid_side // 2, grid_side // 4
    third = mode_count // 2 // (first * second)
    shape = (4, width)
    kind = lax.broadcasted_iota(jnp.int32, shape, 0)
    column = lax.broadcasted_iota(jnp.int32, shape, 1)
    a_odd, b_odd = kind // 2, kind % 2
    a_step = column % (first // 2)
    b_step = column // (first // 2) % (second // 2)
    c_step = column // (first // 2 * (second // 2)) % third
    sine = column // (first // 2 * (second // 2) * third)
    a_index = 2 * a_step + (a_odd + first // 2) % 2
    b_index = 2 * b_step + (b_odd + second // 2) % 2
    row = sine * (mode_count // 2) + c_step * first * second + b_index * first + a_index
    row = jnp.where(column < mode_count // 4, row, -1)
    return a_index - first // 2, b_index - second // 2, c_step + 1, sine, row


def table_factors(grid_side, mode_count, steps, width):
    half = grid_side // 2
    a, b, c, sine, row = class_waves(mode_count, grid_side, width)
    x = jnp.arange(half, dtype=jnp.int32)
    y = jnp.arange(half, dtype=jnp.int32)
    z = jnp.arange(grid_side, dtype=jnp.int32)
    unit = 2.0 * math.pi / grid_side
    scaling = math.sqrt(2.0 / grid_side**3)
    p = jnp.mod(x[:, None, None] * a, grid_side).astype(jnp.float32) * unit
    p = p.reshape(steps, half // steps, 4, width).transpose(0, 2, 1, 3)
    q = jnp.mod(y[:, None, None] * b, grid_side).astype(jnp.float32) * unit
    s = jnp.mod(z[:, None, None] * c, grid_side).astype(jnp.float32) * unit
    size = jnp.where(row >= 0, scaling, 0.0)
    q, s = q.transpose(1, 0, 2)[:, :, None, :], s.transpose(1, 0, 2)[:, None, :, :]
    inner_cos = jnp.cos(q) * jnp.cos(s) - jnp.sin(q) * jnp.sin(s)
    inner_sin = jnp.sin(q) * jnp.cos(s) + jnp.cos(q) * jnp.sin(s)
    is_sine = (sine == 1)[:, None, None, :]
    size = size[:, None, None, :]
    with_cos = jnp.where(is_sine, inner_sin, inner_cos) * size
    with_sin = jnp.where(is_sine, inner_cos, -inner_sin) * size
    flat = (4, 1, half * grid_side, width)
    return jnp.cos(p), jnp.sin(p), with_cos.reshape(flat), with_sin.reshape(flat)


def table_piece(cos_p, sin_p, with_cos, with_sin):
    table = cos_p[:, :, None, :] * with_cos + sin_p[:, :, None, :] * with_sin
    return table.astype(jnp.bfloat16).reshape(4, -1, cos_p.shape[-1])


def column_order(grid_side, mode_count, width):
    row = class_waves(mode_count, grid_side, width)[4].reshape(-1, 1)
    return (row == jnp.arange(mode_count, dtype=jnp.int32)[None, :]).astype(jnp.bfloat16)


def pair_kernel(
    place_ref,
    weight_ref,
    emp_own_ref,
    emp_other_ref,
    order_hbm,
    *refs,
):
    chips = emp_own_ref.shape[0]
    steps = refs[-4].shape[0]
    occ_refs, refs = refs[:chips], refs[chips:]
    tables_hbm, refs = refs[:steps], refs[steps:]
    keep_ref, send_ref = refs[:2]
    raw_occ, raw_emp, occ_wide, emp_wide, first, second, rho, blocks, table, order, table_sem, order_sem = refs[
        2:
    ]
    _, _, depth, width = table.shape
    n_occ, n_rows = raw_occ.shape[1:]
    n_emp = raw_emp.shape[1]
    per_group = 2 * chips // (2 * steps)
    plane = SIDE * SIDE // 2

    used = tables_hbm[0].shape[1]
    table_copies = [
        pltpu.make_async_copy(tables_hbm[s], table.at[s, :, pl.ds(0, used)], table_sem.at[s])
        for s in range(steps)
    ]
    for copy in table_copies:
        copy.start()
    order_copy = pltpu.make_async_copy(order_hbm, order, order_sem)
    order_copy.start()

    core = place_ref[chips]
    me = place_ref[chips + 1]
    for index, ref in enumerate(occ_refs):
        chip = place_ref[index]
        raw_occ[chip * 2 + core] = ref[0]
        raw_occ[chip * 2 + 1 - core] = ref[1]
    for chip in range(chips):
        raw_emp[chip * 2 + core] = emp_own_ref[chip]
        raw_emp[chip * 2 + 1 - core] = emp_other_ref[chip]

    def halves(raw, group, upper):
        pieces = []
        for x in range(3):
            start = (2 * x + upper) * plane
            stop = start + plane
            while start < stop:
                shard, offset = divmod(start, n_rows)
                count = min(stop - start, n_rows - offset)
                rows = raw[group * per_group + shard].astype(jnp.float32)
                pieces.append(rows[:, offset : offset + count])
                start += count
        pieces.append(jnp.zeros((raw.shape[1], depth - 3 * plane), jnp.float32))
        return jnp.concatenate(pieces, axis=1)

    for group in range(2 * steps):
        for upper in range(2):
            occ_wide[group, upper] = halves(raw_occ, group, upper)
            emp_wide[group, upper] = halves(raw_emp, group, upper).astype(jnp.bfloat16)

    rho[...] = jnp.zeros_like(rho)
    for s in range(steps):
        table[s, :, used:, :] = jnp.zeros((4, depth - used, width), jnp.bfloat16)
    quarter = n_occ // 4

    def build(step, target, part):
        sources = [(step, 0), (step, 1), (step + steps, 0), (step + steps, 1)]
        for lane in range(0, depth, LANES):
            cut = slice(lane, lane + LANES)
            occ_rows = [
                occ_wide[group, upper, part * quarter : (part + 1) * quarter, cut] for group, upper in sources
            ]
            emp_rows = [emp_wide[group, upper, :, cut] for group, upper in sources]
            for i in range(quarter):
                near_low, near_high, far_low, far_high = (
                    jnp.broadcast_to(occ_rows[k][i : i + 1], (n_emp, LANES)).astype(jnp.bfloat16) * emp_rows[k]
                    for k in range(4)
                )
                even_low, odd_low = near_low + far_low, near_low - far_low
                even_high, odd_high = near_high + far_high, near_high - far_high
                start = (part * quarter + i) * n_emp
                target[0, start : start + n_emp, cut] = even_low + even_high
                target[1, start : start + n_emp, cut] = even_low - even_high
                target[2, start : start + n_emp, cut] = odd_low + odd_high
                target[3, start : start + n_emp, cut] = odd_low - odd_high

    def multiply(step, source, k):
        rho[k] += jnp.dot(source[k], table[step, k], preferred_element_type=jnp.float32)

    for part in range(4):
        build(0, first, part)

    def two_steps(t, carry):
        for offset, (now, later) in enumerate(((first, second), (second, first))):
            step = 2 * t + offset
            pltpu.make_async_copy(
                tables_hbm[0], table.at[step, :, pl.ds(0, used)], table_sem.at[step]
            ).wait()
            following = lax.rem(step + 1, steps)
            for k in range(4):
                build(following, later, k)
                multiply(step, now, k)
        return carry

    lax.fori_loop(0, steps // 2, two_steps, 0)

    order_copy.wait()
    columns = jnp.concatenate([rho[k].astype(jnp.bfloat16) for k in range(4)], axis=1)
    ordered = jnp.dot(columns, order[...], preferred_element_type=jnp.float32)
    weighted = (ordered * weight_ref[...]).astype(jnp.bfloat16)
    moment = lax.dot_general(
        weighted,
        ordered.astype(jnp.bfloat16),
        (((0,), (0,)), ((), ())),
        preferred_element_type=jnp.float32,
    )
    count, rows = blocks.shape[:2]
    for k in range(count):
        blocks[k] = moment[k * rows : (k + 1) * rows]
    for k in range(count // 2):
        keep_ref[k] = blocks[jnp.bitwise_xor(me, 2 * k)]
        send_ref[k] = blocks[jnp.bitwise_xor(me, 2 * k + 1)].astype(jnp.bfloat16)


def pair_moment(place, weights, occ_blocks, emp_own, emp_other, tables, order):
    chips, n_emp, n_rows = emp_own.shape
    n_occ = occ_blocks[0].shape[1]
    steps = len(tables)
    _, used, width = tables[0].shape
    depth = round_up(used, LANES)
    pairs = n_occ * n_emp
    modes = order.shape[1]
    blocks = 2 * chips
    rows = modes // blocks
    vmem = pl.BlockSpec(memory_space=pltpu.VMEM)
    hbm = pl.BlockSpec(memory_space=pl.ANY)
    return pl.pallas_call(
        pair_kernel,
        out_shape=(
            jax.ShapeDtypeStruct((blocks // 2, rows, modes), jnp.float32),
            jax.ShapeDtypeStruct((blocks // 2, rows, modes), jnp.bfloat16),
        ),
        in_specs=[pl.BlockSpec(memory_space=pltpu.SMEM), vmem, vmem, vmem, hbm]
        + [vmem] * chips
        + [hbm] * steps,
        out_specs=(vmem, vmem),
        scratch_shapes=[
            pltpu.VMEM((2 * chips, n_occ, n_rows), jnp.bfloat16),
            pltpu.VMEM((2 * chips, n_emp, n_rows), jnp.bfloat16),
            pltpu.VMEM((2 * steps, 2, n_occ, depth), jnp.float32),
            pltpu.VMEM((2 * steps, 2, n_emp, depth), jnp.bfloat16),
            pltpu.VMEM((4, pairs, depth), jnp.bfloat16),
            pltpu.VMEM((4, pairs, depth), jnp.bfloat16),
            pltpu.VMEM((4, pairs, width), jnp.float32),
            pltpu.VMEM((blocks, rows, modes), jnp.float32),
            pltpu.VMEM((steps, 4, depth, width), jnp.bfloat16),
            pltpu.VMEM(order.shape, jnp.bfloat16),
            pltpu.SemaphoreType.DMA((steps,)),
            pltpu.SemaphoreType.DMA,
        ],
        compiler_params=pltpu.CompilerParams(vmem_limit_bytes=60 * 1024 * 1024),
        cost_estimate=pl.CostEstimate(
            flops=2 * steps * 4 * pairs * depth * width, bytes_accessed=16 * 2**20, transcendentals=0
        ),
        name="pair_moment",
    )(place, weights, emp_own, emp_other, order, *occ_blocks, *tables)


def ring_of(chips):
    return list(range(0, chips, 2)) + list(range(chips - 1, 0, -2))


def gather_ring(block, chips, between):
    ring = ring_of(chips)
    ahead, back = [], []
    for position in range(chips):
        for core in range(2):
            here = 2 * ring[position] + core
            right = 2 * ring[(position + 1) % chips] + core
            ahead.append((here, right))
            back.append((right, here))
    found, offsets, made = [block], [0], []
    from_left = from_right = block
    for hop in range(1, chips // 2 + 1):
        if hop <= len(between):
            function, arguments = between[hop - 1]
            (from_left, from_right), arguments = lax.optimization_barrier(((from_left, from_right), arguments))
            made.append(function(*arguments))
        from_left = lax.ppermute(from_left, "space", ahead)
        found.append(from_left)
        offsets.append(-hop)
        if 2 * hop < chips:
            from_right = lax.ppermute(from_right, "space", back)
            found.append(from_right)
            offsets.append(hop)
    return found, offsets, made


def local(space, tm, orbitals, gaps, times, cos_weights):
    rows = orbitals.shape[0]
    chips = space // 2
    columns = orbitals.T
    own_occ, own_emp = NOCC // 2, NEMP // chips
    me = lax.axis_index("space")
    core, chip = me % 2, me // 2
    swap = [(d, d ^ 1) for d in range(space)]

    occ = columns[:NOCC].reshape(2, own_occ, rows)
    occ_mine = lax.dynamic_index_in_dim(occ, core, 0, keepdims=False)
    occ_theirs = lax.dynamic_index_in_dim(occ, 1 - core, 0, keepdims=False)
    occ_pair = jnp.stack([occ_mine, lax.ppermute(occ_theirs, "space", swap)])
    emp_own = lax.all_to_all(
        columns[NOCC:].reshape(chips, own_emp, rows),
        "space",
        split_axis=0,
        concat_axis=0,
        axis_index_groups=[[2 * k + c for k in range(chips)] for c in range(2)],
    )
    planes = 3
    steps = SIDE // 2 // planes
    width = round_up(NG // 4, 2 * LANES)
    cos_p, sin_p, with_cos, with_sin = table_factors(SIDE, NG, steps, width)
    between = [(table_piece, (cos_p[k], sin_p[k], with_cos, with_sin)) for k in range(steps)]
    occ_blocks, offsets, tables = gather_ring(occ_pair, chips, between)
    emp_other = lax.ppermute(emp_own, "space", swap)
    order = column_order(SIDE, NG, width)

    position = jnp.where(chip % 2 == 0, chip // 2, chips - (chip + 1) // 2)
    places = (position + jnp.array(offsets, jnp.int32)) % chips
    on_ring = jnp.where(places < chips // 2, 2 * places, 2 * (chips - places) - 1)
    place = jnp.concatenate([on_ring, jnp.stack([core, me])]).astype(jnp.int32)

    own_count = cos_weights.shape[0] // tm
    tm_index = lax.axis_index("tm")
    pair_weights = 0.0
    for hop in range(tm):
        source = (tm_index + hop) % tm
        their_times = times
        if hop:
            their_times = lax.ppermute(times, "tm", [((d + hop) % tm, d) for d in range(tm)])
        factors = jnp.exp(-gaps[None, :] * their_times[:, None])
        occ_factors = lax.dynamic_slice_in_dim(factors, core * own_occ, own_occ, 1) * NOCC ** (-0.5)
        emp_factors = lax.dynamic_slice_in_dim(factors, NOCC + chip * own_emp, own_emp, 1) * NEMP ** (-0.5)
        weights = lax.dynamic_slice(
            cos_weights,
            (tm_index * own_count, source * times.shape[0]),
            (own_count, times.shape[0]),
        )
        pair_weights = pair_weights + jnp.sum(
            weights[:, :, None, None] * (occ_factors[:, :, None] * emp_factors[:, None, :])[None], axis=1
        )
    pair_weights = pair_weights.reshape(own_count, own_occ * own_emp, 1)

    results = []
    for w in range(own_count):
        keep, send = pair_moment(place, pair_weights[w], occ_blocks, emp_own, emp_other, tables, order)
        received = lax.ppermute(send, "space", swap)
        total = keep + received.astype(jnp.float32)
        parts = total.astype(jnp.bfloat16)
        result = total[0]
        for distance in range(1, chips):
            part = lax.ppermute(
                parts[distance], "space", [(d, d ^ (2 * distance)) for d in range(space)]
            )
            result = result + part.astype(jnp.float32)
        results.append(result)
    return jnp.stack(results)


def solution(mesh):
    return jax.shard_map(
        functools.partial(local, mesh.shape["space"], mesh.shape["tm"]),
        mesh=mesh,
        in_specs=(P("space", None), P(), P("tm"), P()),
        out_specs=P("tm", "space", None),
        check_vma=False,
    )
```

```python
import functools
import math

import jax
import jax.numpy as jnp
from jax import lax
from jax.experimental import pallas as pl
from jax.experimental.pallas import tpu as pltpu
from jax.sharding import PartitionSpec as P

SIDE = 24
NG = 864
NOCC = 64
NEMP = 256
LANES = 128


def round_up(value, step):
    return -(-value // step) * step


def class_waves(mode_count, grid_side, width, zero):
    first, second = grid_side // 2, grid_side // 4
    third = mode_count // 2 // (first * second)
    shape = (4, width)
    kind = lax.broadcasted_iota(jnp.int32, shape, 0)
    column = lax.broadcasted_iota(jnp.int32, shape, 1) + zero
    a_odd, b_odd = kind // 2, kind % 2
    b_step = column % (second // 2)
    c_step = column // (second // 2) % third
    sine = column // (second // 2 * third) % 2
    a_step = column // (second // 2 * third * 2)
    a_index = 2 * a_step + (a_odd + first // 2) % 2
    b_index = 2 * b_step + (b_odd + second // 2) % 2
    return a_index - first // 2, b_index - second // 2, c_step + 1, sine, column < mode_count // 4


def table_factors(grid_side, mode_count, steps, width, zero):
    half = grid_side // 2
    a, b, c, sine, used = class_waves(mode_count, grid_side, width, zero)
    x = jnp.arange(half, dtype=jnp.int32)
    y = jnp.arange(half, dtype=jnp.int32)
    z = jnp.arange(grid_side, dtype=jnp.int32)
    unit = 2.0 * math.pi / grid_side
    scaling = math.sqrt(2.0 / grid_side**3)
    p = jnp.mod(x[:, None, None] * a, grid_side).astype(jnp.float32) * unit
    p = p.reshape(steps, half // steps, 4, width).transpose(0, 2, 1, 3)
    q = jnp.mod(y[:, None, None] * b, grid_side).astype(jnp.float32) * unit
    s = jnp.mod(z[:, None, None] * c, grid_side).astype(jnp.float32) * unit
    size = jnp.where(used, scaling, 0.0)
    q, s = q.transpose(1, 0, 2)[:, :, None, :], s.transpose(1, 0, 2)[:, None, :, :]
    inner_cos = jnp.cos(q) * jnp.cos(s) - jnp.sin(q) * jnp.sin(s)
    inner_sin = jnp.sin(q) * jnp.cos(s) + jnp.cos(q) * jnp.sin(s)
    is_sine = (sine == 1)[:, None, None, :]
    size = size[:, None, None, :]
    with_cos = jnp.where(is_sine, inner_sin, inner_cos) * size
    with_sin = jnp.where(is_sine, inner_cos, -inner_sin) * size
    flat = (4, 1, half * grid_side, width)
    return jnp.cos(p), jnp.sin(p), with_cos.reshape(flat), with_sin.reshape(flat)


def table_piece(cos_p, sin_p, with_cos, with_sin):
    table = cos_p[:, :, None, :] * with_cos + sin_p[:, :, None, :] * with_sin
    return table.astype(jnp.bfloat16).reshape(4, -1, cos_p.shape[-1])


def pair_kernel(place_ref, weight_ref, emp_own_ref, emp_other_ref, *refs):
    table, table_sem = refs[-2:]
    steps = table_sem.shape[0]
    chips = emp_own_ref.shape[0]
    occ_refs, refs = refs[:chips], refs[chips:]
    tables_hbm, refs = refs[:steps], refs[steps:]
    keep_ref, send_ref, raw_occ, occ_wide, emp_wide, first, second, rho = refs[:-2]
    width = table.shape[2]
    depth = table.shape[1] // steps
    n_occ, n_rows = raw_occ.shape[1:]
    n_emp = emp_own_ref.shape[1]
    per_group = chips // steps
    plane = SIDE * SIDE // 2
    half_pairs = first.shape[1]
    half_occ = n_occ // 2

    used = tables_hbm[0].shape[1]
    copies = [
        pltpu.make_async_copy(tables_hbm[s], table.at[:, pl.ds(s * depth, used)], table_sem.at[s])
        for s in range(steps)
    ]
    for copy in copies:
        copy.start()

    core = place_ref[chips]
    me = place_ref[chips + 1]
    for index, ref in enumerate(occ_refs):
        chip = place_ref[index]
        raw_occ[chip * 2 + core] = ref[0]
        raw_occ[chip * 2 + 1 - core] = ref[1]

    def occ_rows_of(shard):
        return raw_occ[shard].astype(jnp.float32)

    def emp_rows_of(shard):
        own = emp_own_ref[shard // 2].astype(jnp.float32)
        other = emp_other_ref[shard // 2].astype(jnp.float32)
        return jnp.where(core == shard % 2, own, other)

    def halves(rows_of, columns, group, upper):
        pieces = []
        for x in range(3):
            start = (2 * x + upper) * plane
            stop = start + plane
            while start < stop:
                shard, offset = divmod(start, n_rows)
                count = min(stop - start, n_rows - offset)
                pieces.append(rows_of(group * per_group + shard)[:, offset : offset + count])
                start += count
        pieces.append(jnp.zeros((columns, depth - 3 * plane), jnp.float32))
        return jnp.concatenate(pieces, axis=1)

    for far in range(2):
        for step in range(steps):
            lanes = slice(step * depth, (step + 1) * depth)
            for upper in range(2):
                group = far * steps + step
                occ_wide[2 * far + upper, :, lanes] = halves(occ_rows_of, n_occ, group, upper)
                emp_wide[2 * far + upper, :, lanes] = halves(emp_rows_of, n_emp, group, upper).astype(
                    jnp.bfloat16
                )
    for step in range(steps):
        table[:, step * depth + used : (step + 1) * depth, :] = jnp.zeros(
            (4, depth - used, width), jnp.bfloat16
        )

    def build(half, target, cut):
        occ_rows = [occ_wide[k, half * half_occ : (half + 1) * half_occ, cut] for k in range(4)]
        emp_rows = [emp_wide[k, :, cut] for k in range(4)]
        for i in range(half_occ):
            near_low, near_high, far_low, far_high = (
                jnp.broadcast_to(occ_rows[k][i : i + 1], (n_emp, LANES)).astype(jnp.bfloat16) * emp_rows[k]
                for k in range(4)
            )
            even_low, odd_low = near_low + far_low, near_low - far_low
            even_high, odd_high = near_high + far_high, near_high - far_high
            rows = slice(i * n_emp, (i + 1) * n_emp)
            target[0, rows, cut] = even_low + even_high
            target[1, rows, cut] = even_low - even_high
            target[2, rows, cut] = odd_low + odd_high
            target[3, rows, cut] = odd_low - odd_high

    modes = rho.shape[1]
    spacing = SIDE
    per_a = modes // spacing

    def multiply(half, source, k):
        found = jnp.dot(source[k], table[k], preferred_element_type=jnp.float32).T
        a_odd, b_odd = divmod(k, 2)
        a_first = (a_odd + SIDE // 4) % 2
        b_first = (b_odd + SIDE // 8) % 2
        for a_step in range(SIDE // 4):
            start = b_first * (SIDE // 2) + 2 * a_step + a_first
            for tile in range(half_pairs // LANES):
                rho[half * half_pairs // LANES + tile, pl.ds(start, per_a, stride=spacing), :] = found[
                    a_step * per_a : (a_step + 1) * per_a, tile * LANES : (tile + 1) * LANES
                ]

    chunks = steps * depth // LANES

    def build_first(chunk, carry):
        build(0, first, pl.ds(pl.multiple_of(chunk * LANES, LANES), LANES))
        return carry

    lax.fori_loop(0, chunks, build_first, 0)
    for copy in copies:
        copy.wait()
    for k in range(4):
        for chunk in range(k * chunks // 4, (k + 1) * chunks // 4):
            build(1, second, slice(chunk * LANES, (chunk + 1) * LANES))
        multiply(0, first, k)
    for k in range(4):
        multiply(1, second, k)

    tiles = range(rho.shape[0])
    ordered = jnp.concatenate([rho[tile].astype(jnp.bfloat16) for tile in tiles], axis=1)
    weighted = jnp.concatenate(
        [
            (rho[tile] * weight_ref[:, tile * LANES : (tile + 1) * LANES]).astype(jnp.bfloat16)
            for tile in tiles
        ],
        axis=1,
    )
    moment = lax.dot_general(
        weighted, ordered, (((1,), (1,)), ((), ())), preferred_element_type=jnp.float32
    )
    count, rows = 2 * chips, keep_ref.shape[1]
    for own_core in range(2):

        @pl.when(core == own_core)
        def _():
            for k in range(count):
                slot = jnp.bitwise_xor(me, k) // 2
                block = moment[k * rows : (k + 1) * rows]
                if k % 2 == own_core:
                    keep_ref[slot] = block
                else:
                    send_ref[slot] = block.astype(jnp.bfloat16)


def pair_moment(place, weights, occ_blocks, emp_own, emp_other, tables):
    chips, n_emp, n_rows = emp_own.shape
    n_occ = occ_blocks[0].shape[1]
    steps = len(tables)
    _, used, width = tables[0].shape
    depth = round_up(used, LANES)
    pairs = n_occ * n_emp
    blocks = 2 * chips
    rows = NG // blocks
    vmem = pl.BlockSpec(memory_space=pltpu.VMEM)
    hbm = pl.BlockSpec(memory_space=pl.ANY)
    return pl.pallas_call(
        pair_kernel,
        out_shape=(
            jax.ShapeDtypeStruct((blocks // 2, rows, NG), jnp.float32),
            jax.ShapeDtypeStruct((blocks // 2, rows, NG), jnp.bfloat16),
        ),
        in_specs=[pl.BlockSpec(memory_space=pltpu.SMEM), vmem, vmem, vmem] + [vmem] * chips + [hbm] * steps,
        out_specs=(vmem, vmem),
        scratch_shapes=[
            pltpu.VMEM((2 * chips, n_occ, n_rows), jnp.bfloat16),
            pltpu.VMEM((4, n_occ, steps * depth), jnp.float32),
            pltpu.VMEM((4, n_emp, steps * depth), jnp.bfloat16),
            pltpu.VMEM((4, pairs // 2, steps * depth), jnp.bfloat16),
            pltpu.VMEM((4, pairs // 2, steps * depth), jnp.bfloat16),
            pltpu.VMEM((pairs // LANES, NG, LANES), jnp.float32),
            pltpu.VMEM((4, steps * depth, width), jnp.bfloat16),
            pltpu.SemaphoreType.DMA((steps,)),
        ],
        compiler_params=pltpu.CompilerParams(vmem_limit_bytes=60 * 1024 * 1024),
        cost_estimate=pl.CostEstimate(
            flops=2 * steps * 4 * pairs * depth * width, bytes_accessed=16 * 2**20, transcendentals=0
        ),
        name="pair_moment",
    )(place, weights, emp_own, emp_other, *occ_blocks, *tables)


def ring_of(chips):
    return list(range(0, chips, 2)) + list(range(chips - 1, 0, -2))


def gather_ring(block, chips, between):
    ring = ring_of(chips)
    ahead, back = [], []
    for position in range(chips):
        for core in range(2):
            here = 2 * ring[position] + core
            right = 2 * ring[(position + 1) % chips] + core
            ahead.append((here, right))
            back.append((right, here))
    found, offsets, made = [block], [0], []
    from_left = from_right = block
    for hop in range(1, chips // 2 + 1):
        if hop <= len(between):
            function, arguments = between[hop - 1]
            if hop > 1:
                _, arguments = lax.optimization_barrier((from_left, arguments))
            made.append(function(*arguments))
        from_left = lax.ppermute(from_left, "space", ahead)
        found.append(from_left)
        offsets.append(-hop)
        if 2 * hop < chips:
            from_right = lax.ppermute(from_right, "space", back)
            found.append(from_right)
            offsets.append(hop)
    return found, offsets, made


def local(space, tm, orbitals, gaps, times, cos_weights):
    rows = orbitals.shape[0]
    chips = space // 2
    columns = orbitals.T
    own_occ, own_emp = NOCC // 2, NEMP // chips
    me = lax.axis_index("space")
    core, chip = me % 2, me // 2
    swap = [(d, d ^ 1) for d in range(space)]

    occ = columns[:NOCC].reshape(2, own_occ, rows)
    occ_mine = lax.dynamic_index_in_dim(occ, core, 0, keepdims=False)
    occ_theirs = lax.dynamic_index_in_dim(occ, 1 - core, 0, keepdims=False)
    occ_pair = jnp.stack([occ_mine, lax.ppermute(occ_theirs, "space", swap)])
    emp_own = lax.all_to_all(
        columns[NOCC:].reshape(chips, own_emp, rows),
        "space",
        split_axis=0,
        concat_axis=0,
        axis_index_groups=[[2 * k + c for k in range(chips)] for c in range(2)],
    )
    _, gaps, cos_weights, zero = lax.optimization_barrier((occ_pair, gaps, cos_weights, jnp.int32(0)))
    planes = 3
    steps = SIDE // 2 // planes
    width = round_up(NG // 4, 2 * LANES)
    cos_p, sin_p, with_cos, with_sin = table_factors(SIDE, NG, steps, width, zero)
    between = [(table_piece, (cos_p[k], sin_p[k], with_cos, with_sin)) for k in range(steps)]
    occ_blocks, offsets, tables = gather_ring(occ_pair, chips, between)
    emp_other = lax.ppermute(emp_own, "space", swap)

    position = jnp.where(chip % 2 == 0, chip // 2, chips - (chip + 1) // 2)
    places = (position + jnp.array(offsets, jnp.int32) + zero) % chips
    on_ring = jnp.where(places < chips // 2, 2 * places, 2 * (chips - places) - 1)
    place = jnp.concatenate([on_ring, jnp.stack([core, me])]).astype(jnp.int32)

    own_count = cos_weights.shape[0] // tm
    tm_index = lax.axis_index("tm")
    pair_weights = 0.0
    for hop in range(tm):
        source = (tm_index + hop) % tm
        their_times = times
        if hop:
            their_times = lax.ppermute(times, "tm", [((d + hop) % tm, d) for d in range(tm)])
        factors = jnp.exp(-gaps[None, :] * their_times[:, None])
        occ_factors = lax.dynamic_slice_in_dim(factors, core * own_occ, own_occ, 1) * NOCC ** (-0.5)
        emp_factors = lax.dynamic_slice_in_dim(factors, NOCC + chip * own_emp, own_emp, 1) * NEMP ** (-0.5)
        weights = lax.dynamic_slice(
            cos_weights,
            (tm_index * own_count, source * times.shape[0]),
            (own_count, times.shape[0]),
        )
        pair_weights = pair_weights + jnp.sum(
            weights[:, :, None, None] * (occ_factors[:, :, None] * emp_factors[:, None, :])[None], axis=1
        )
    pair_weights = pair_weights.reshape(own_count, 1, own_occ * own_emp)

    results = []
    for w in range(own_count):
        keep, send = pair_moment(place, pair_weights[w], occ_blocks, emp_own, emp_other, tables)
        received = lax.ppermute(send, "space", swap)
        total = keep + received.astype(jnp.float32)
        parts = total.astype(jnp.bfloat16)
        result = total[0]
        for distance in range(1, chips):
            part = lax.ppermute(
                parts[distance], "space", [(d, d ^ (2 * distance)) for d in range(space)]
            )
            result = result + part.astype(jnp.float32)
        results.append(result)
    return jnp.stack(results)


def solution(mesh):
    return jax.shard_map(
        functools.partial(local, mesh.shape["space"], mesh.shape["tm"]),
        mesh=mesh,
        in_specs=(P("space", None), P(), P("tm"), P()),
        out_specs=P("tm", "space", None),
        check_vma=False,
    )
```

```python
import functools
import math

import jax
import jax.numpy as jnp
from jax import lax
from jax.experimental import pallas as pl
from jax.experimental.pallas import tpu as pltpu
from jax.sharding import PartitionSpec as P

SIDE = 24
NG = 864
NOCC = 64
NEMP = 256
LANES = 128
PLANES = 3


def round_up(value, step):
    return -(-value // step) * step


def pair_weights(tm, n_occ, n_emp, own_count, times_refs, gaps_ref, cos_ref, out_ref):
    me = lax.axis_index("space")
    tm_index = lax.axis_index("tm")
    core, own_chip = me % 2, me // 2
    shape = out_ref.shape[1:]
    pair = lax.broadcasted_iota(jnp.int32, shape, 0) * LANES + lax.broadcasted_iota(jnp.int32, shape, 1)
    emp_number = lax.rem(pair, n_emp)
    occ_gap = jnp.zeros(shape, jnp.float32)
    emp_gap = jnp.zeros(shape, jnp.float32)
    for i in range(n_occ):
        occ_gap = jnp.where(pair >= i * n_emp, gaps_ref[core * n_occ + i], occ_gap)
    for j in range(n_emp):
        emp_gap = jnp.where(emp_number == j, gaps_ref[NOCC + own_chip * n_emp + j], emp_gap)
    for w in range(own_count):
        weights = jnp.zeros(shape, jnp.float32)
        for hop, times_ref in enumerate(times_refs):
            source = lax.rem(tm_index + hop, tm)
            for k in range(times_ref.shape[0]):
                occ_factor = jnp.exp(-occ_gap * times_ref[k]) * NOCC ** (-0.5)
                emp_factor = jnp.exp(-emp_gap * times_ref[k]) * NEMP ** (-0.5)
                share = cos_ref[tm_index * own_count + w, source * times_ref.shape[0] + k]
                weights = weights + share * (occ_factor * emp_factor)
        out_ref[w] = weights


def table_kernel(held_ref, out_ref, with_cos, with_sin):
    kind = pl.program_id(0) + held_ref[0]
    a_odd, b_odd = kind // 2, kind % 2
    half = SIDE // 2
    a_waves, b_waves, c_waves = SIDE // 4, SIDE // 8, NG // (SIDE // 2 * (SIDE // 4) * 2)
    width = out_ref.shape[2]

    def parts(value, size):
        whole = jnp.floor((value + 0.5) * (1.0 / size))
        return whole, value - size * whole

    column = lax.broadcasted_iota(jnp.int32, (SIDE, width), 1).astype(jnp.float32)
    row = lax.broadcasted_iota(jnp.int32, (SIDE, width), 0).astype(jnp.float32)
    a_step, rest = parts(column, 2 * c_waves * b_waves)
    sine, rest = parts(rest, c_waves * b_waves)
    c_step, b_step = parts(rest, b_waves)
    a = 2.0 * a_step + ((a_odd + a_waves) % 2 - a_waves).astype(jnp.float32)
    b = 2.0 * b_step + ((b_odd + b_waves) % 2 - b_waves).astype(jnp.float32)
    c = c_step + 1.0
    unit = 2.0 * math.pi / SIDE
    size = jnp.where(a_step < a_waves, math.sqrt(2.0 / SIDE**3), 0.0)

    def factors(wave):
        angle = parts(wave * row, SIDE)[1] * unit
        return jnp.cos(angle), jnp.sin(angle)

    cos_p, sin_p = factors(a)
    cos_q, sin_q = factors(b)
    cos_s, sin_s = factors(c)
    is_sine = sine > 0.5
    for y in range(half):
        inner_cos = cos_q[y : y + 1] * cos_s - sin_q[y : y + 1] * sin_s
        inner_sin = sin_q[y : y + 1] * cos_s + cos_q[y : y + 1] * sin_s
        rows = slice(y * SIDE, (y + 1) * SIDE)
        with_cos[rows] = jnp.where(is_sine, inner_sin, inner_cos) * size
        with_sin[rows] = jnp.where(is_sine, inner_cos, -inner_sin) * size
    plane = half * SIDE
    depth = round_up(PLANES * plane, LANES)
    for x in range(half):
        start = x // PLANES * depth + x % PLANES * plane
        table = cos_p[x : x + 1] * with_cos[...] + sin_p[x : x + 1] * with_sin[...]
        out_ref[0, start : start + plane] = table.astype(jnp.bfloat16)
    for step in range(half // PLANES):
        out_ref[0, step * depth + PLANES * plane : (step + 1) * depth] = jnp.zeros(
            (depth - PLANES * plane, width), jnp.bfloat16
        )


def prepare_kernel(tm, n_occ, n_emp, own_count, held_ref, *refs):
    times_refs, (gaps_ref, cos_ref, table_ref, weight_ref, with_cos, with_sin) = refs[:tm], refs[tm:]

    @pl.when(pl.program_id(0) == 0)
    def _():
        pair_weights(tm, n_occ, n_emp, own_count, times_refs, gaps_ref, cos_ref, weight_ref)

    table_kernel(held_ref, table_ref, with_cos, with_sin)


def prepare(held, every_time, gaps, cos_weights, n_occ, n_emp):
    plane = SIDE * SIDE // 2
    depth = SIDE // 2 // PLANES * round_up(PLANES * plane, LANES)
    width = round_up(NG // 4, 2 * LANES)
    tm = len(every_time)
    own_count = cos_weights.shape[0] // tm
    weight_shape = (own_count, n_occ * n_emp // LANES, LANES)
    return pl.pallas_call(
        functools.partial(prepare_kernel, tm, n_occ, n_emp, own_count),
        grid=(4,),
        out_shape=(
            jax.ShapeDtypeStruct((4, depth, width), jnp.bfloat16),
            jax.ShapeDtypeStruct(weight_shape, jnp.float32),
        ),
        in_specs=[pl.BlockSpec(memory_space=pltpu.SMEM)] * (tm + 3),
        out_specs=(
            pl.BlockSpec((1, depth, width), lambda k: (k, 0, 0)),
            pl.BlockSpec(weight_shape, lambda k: (0, 0, 0)),
        ),
        scratch_shapes=[pltpu.VMEM((plane, width), jnp.float32), pltpu.VMEM((plane, width), jnp.float32)],
        compiler_params=pltpu.CompilerParams(vmem_limit_bytes=60 * 1024 * 1024),
        cost_estimate=pl.CostEstimate(
            flops=64 * depth * width, bytes_accessed=8 * depth * width, transcendentals=0
        ),
        name="prepare",
    )(held, *every_time, gaps, cos_weights)


def ring_place(chip, chips):
    return jnp.where(chip % 2 == 0, chip // 2, chips - (chip + 1) // 2)


def ring_chip(place, chips):
    place = lax.rem(place + chips, chips)
    return jnp.where(place < chips // 2, 2 * place, 2 * (chips - place) - 1)


def far_slots(chips):
    return [chips // 2, chips // 2 + 1]


def pair_kernel(offsets, weight_ref, emp_own_ref, emp_other_ref, *refs):
    chips = emp_own_ref.shape[0]
    occ_refs, refs = refs[:chips], refs[chips:]
    table_hbm, keep_far, send_far, keep_near, send_near = refs[:5]
    raw_occ, occ_wide, emp_wide, first, second, rho, blocks, table, table_sem = refs[5:]
    depth = round_up(PLANES * SIDE * SIDE // 2, LANES)
    steps = table.shape[1] // depth
    n_occ, n_rows = raw_occ.shape[1:]
    n_emp = emp_own_ref.shape[1]
    per_group = chips // steps
    plane = SIDE * SIDE // 2
    half_pairs = first.shape[1]
    half_occ = n_occ // 2

    copies = [pltpu.make_async_copy(table_hbm.at[k], table.at[k], table_sem.at[k]) for k in range(4)]
    for copy in copies:
        copy.start()

    me = lax.axis_index("space")
    core, own_chip = me % 2, me // 2
    place = ring_place(own_chip, chips)
    for offset, ref in zip(offsets, occ_refs, strict=True):
        chip = ring_chip(place + offset, chips)
        raw_occ[chip * 2 + core] = ref[0]
        raw_occ[chip * 2 + 1 - core] = ref[1]

    def occ_rows_of(shard):
        return raw_occ[shard].astype(jnp.float32)

    def emp_rows_of(shard):
        own = emp_own_ref[shard // 2].astype(jnp.float32)
        other = emp_other_ref[shard // 2].astype(jnp.float32)
        return jnp.where(core == shard % 2, own, other)

    def halves(rows_of, columns, group, upper):
        pieces = []
        for x in range(PLANES):
            start = (2 * x + upper) * plane
            stop = start + plane
            while start < stop:
                shard, offset = divmod(start, n_rows)
                count = min(stop - start, n_rows - offset)
                pieces.append(rows_of(group * per_group + shard)[:, offset : offset + count])
                start += count
        pieces.append(jnp.zeros((columns, depth - PLANES * plane), jnp.float32))
        return jnp.concatenate(pieces, axis=1)

    for far in range(2):
        for step in range(steps):
            lanes = slice(step * depth, (step + 1) * depth)
            for upper in range(2):
                group = far * steps + step
                occ_wide[2 * far + upper, :, lanes] = halves(occ_rows_of, n_occ, group, upper)
                emp_wide[2 * far + upper, :, lanes] = halves(emp_rows_of, n_emp, group, upper).astype(
                    jnp.bfloat16
                )
    def build(half, target, cut):
        occ_rows = [occ_wide[k, half * half_occ : (half + 1) * half_occ, cut] for k in range(4)]
        emp_rows = [emp_wide[k, :, cut] for k in range(4)]
        for i in range(half_occ):
            near_low, near_high, far_low, far_high = (
                jnp.broadcast_to(occ_rows[k][i : i + 1], (n_emp, LANES)).astype(jnp.bfloat16) * emp_rows[k]
                for k in range(4)
            )
            even_low, odd_low = near_low + far_low, near_low - far_low
            even_high, odd_high = near_high + far_high, near_high - far_high
            rows = slice(i * n_emp, (i + 1) * n_emp)
            target[0, rows, cut] = even_low + even_high
            target[1, rows, cut] = even_low - even_high
            target[2, rows, cut] = odd_low + odd_high
            target[3, rows, cut] = odd_low - odd_high

    modes = rho.shape[1]
    spacing = SIDE
    per_a = modes // spacing

    def multiply(half, source, k):
        found = jnp.dot(source[k], table[k], preferred_element_type=jnp.float32).T
        a_odd, b_odd = divmod(k, 2)
        a_first = (a_odd + SIDE // 4) % 2
        b_first = (b_odd + SIDE // 8) % 2
        for a_step in range(SIDE // 4):
            start = b_first * (SIDE // 2) + 2 * a_step + a_first
            for tile in range(half_pairs // LANES):
                rho[half * half_pairs // LANES + tile, pl.ds(start, per_a, stride=spacing), :] = found[
                    a_step * per_a : (a_step + 1) * per_a, tile * LANES : (tile + 1) * LANES
                ]

    chunks = steps * depth // LANES

    def build_first(chunk, carry):
        build(0, first, pl.ds(pl.multiple_of(chunk * LANES, LANES), LANES))
        return carry

    lax.fori_loop(0, chunks, build_first, 0)
    for k in range(4):
        copies[k].wait()
        for chunk in range(k * chunks // 4, (k + 1) * chunks // 4):
            build(1, second, slice(chunk * LANES, (chunk + 1) * LANES))
        multiply(0, first, k)
    for k in range(4):
        multiply(1, second, k)

    tiles = range(rho.shape[0])
    ordered = jnp.concatenate([rho[tile].astype(jnp.bfloat16) for tile in tiles], axis=1)
    weighted = jnp.concatenate(
        [
            (rho[tile] * weight_ref[tile : tile + 1]).astype(jnp.bfloat16) for tile in tiles
        ],
        axis=1,
    )
    moment = lax.dot_general(
        weighted, ordered, (((1,), (1,)), ((), ())), preferred_element_type=jnp.float32
    )
    rows = blocks.shape[1]
    for k in range(2 * chips):
        blocks[k] = moment[k * rows : (k + 1) * rows]
    far = far_slots(chips)
    near = [slot for slot in range(chips) if slot not in far]
    for slots, keep, send in ((far, keep_far, send_far), (near, keep_near, send_near)):
        for index, slot in enumerate(slots):
            chip = ring_chip(place + slot, chips)
            start = index * round_up(rows, 16)
            keep[start : start + rows, :NG] = blocks[2 * chip + core]
            send[start : start + rows, :NG] = blocks[2 * chip + 1 - core].astype(jnp.bfloat16)


def pair_moment(weights, occ_blocks, offsets, emp_own, emp_other, tables):
    chips, n_emp, n_rows = emp_own.shape
    n_occ = occ_blocks[0].shape[1]
    _, depth, width = tables.shape
    pairs = n_occ * n_emp
    rows = NG // (2 * chips)
    far_rows, near_rows = 2 * round_up(rows, 16), (chips - 2) * round_up(rows, 16)
    vmem = pl.BlockSpec(memory_space=pltpu.VMEM)
    return pl.pallas_call(
        functools.partial(pair_kernel, offsets),
        out_shape=tuple(
            jax.ShapeDtypeStruct((count, round_up(NG, LANES)), dtype)
            for count in (far_rows, near_rows)
            for dtype in (jnp.float32, jnp.bfloat16)
        ),
        in_specs=[vmem] * (3 + chips) + [pl.BlockSpec(memory_space=pl.ANY)],
        out_specs=(vmem, vmem, vmem, vmem),
        scratch_shapes=[
            pltpu.VMEM((2 * chips, n_occ, n_rows), jnp.bfloat16),
            pltpu.VMEM((4, n_occ, depth), jnp.float32),
            pltpu.VMEM((4, n_emp, depth), jnp.bfloat16),
            pltpu.VMEM((4, pairs // 2, depth), jnp.bfloat16),
            pltpu.VMEM((4, pairs // 2, depth), jnp.bfloat16),
            pltpu.VMEM((pairs // LANES, NG, LANES), jnp.float32),
            pltpu.VMEM((2 * chips, rows, NG), jnp.float32),
            pltpu.VMEM((4, depth, width), jnp.bfloat16),
            pltpu.SemaphoreType.DMA((4,)),
        ],
        compiler_params=pltpu.CompilerParams(vmem_limit_bytes=60 * 1024 * 1024),
        cost_estimate=pl.CostEstimate(
            flops=8 * pairs * depth * width, bytes_accessed=16 * 2**20, transcendentals=0
        ),
        name="pair_moment",
    )(weights, emp_own, emp_other, *occ_blocks, tables)


def ring_steps(chips):
    ring = list(range(0, chips, 2)) + list(range(chips - 1, 0, -2))
    ahead = [
        (2 * ring[k] + core, 2 * ring[(k + 1) % chips] + core) for k in range(chips) for core in range(2)
    ]
    return ahead, [(to, start) for start, to in ahead]


def hold(value, until):
    return lax.optimization_barrier((value, until))[0]


def gather_ring(block, chips, work, beside):
    ahead, back = ring_steps(chips)
    found, offsets = [block], [0]
    from_left = from_right = block
    for hop in range(1, chips // 2 + 1):
        if hop == 3:
            from_left, from_right, made, beside = lax.optimization_barrier(
                (from_left, from_right, made, beside)
            )
        elif hop > 1:
            from_left, from_right = lax.optimization_barrier((from_left, from_right))
        from_left = lax.ppermute(from_left, "space", ahead)
        found.append(from_left)
        offsets.append(-hop)
        if 2 * hop < chips:
            from_right = lax.ppermute(from_right, "space", back)
            found.append(from_right)
            offsets.append(hop)
        if hop == 1:
            made = work(from_left)
    return found, offsets, made, beside


def reduce_ring(totals, chips):
    ahead, back = ring_steps(chips)
    farthest = chips // 2
    from_left, from_right = totals[farthest], totals[farthest + 1]
    for hop in range(1, farthest + 1):
        from_left = lax.ppermute(from_left.astype(jnp.bfloat16), "space", ahead).astype(jnp.float32)
        if hop < farthest:
            from_right = lax.ppermute(from_right.astype(jnp.bfloat16), "space", back).astype(jnp.float32)
            from_left = from_left + totals[farthest - hop]
        if hop < farthest - 1:
            from_right = from_right + totals[farthest + 1 + hop]
    return (totals[0] + from_left + from_right)[:, :NG]


def local(space, tm, orbitals, gaps, times, cos_weights):
    rows = orbitals.shape[0]
    chips = space // 2
    columns = orbitals.T
    own_occ, own_emp = NOCC // 2, NEMP // chips
    core = lax.axis_index("space") % 2
    swap = [(d, d ^ 1) for d in range(space)]

    occ = columns[:NOCC].reshape(2, own_occ, rows)
    occ_mine = lax.dynamic_index_in_dim(occ, core, 0, keepdims=False)
    occ_theirs = lax.dynamic_index_in_dim(occ, 1 - core, 0, keepdims=False)
    occ_pair = jnp.stack([occ_mine, lax.ppermute(occ_theirs, "space", swap)])
    emp_own = lax.all_to_all(
        columns[NOCC:].reshape(chips, own_emp, rows),
        "space",
        split_axis=0,
        concat_axis=0,
        axis_index_groups=[[2 * k + c for k in range(chips)] for c in range(2)],
    )
    every_time = [times] + [
        lax.ppermute(times, "tm", [((d + hop) % tm, d) for d in range(tm)]) for hop in range(1, tm)
    ]

    def work(block):
        held = hold(jnp.zeros((1,), jnp.int32), block)
        return prepare(held, every_time, gaps, cos_weights, own_occ, own_emp)

    occ_blocks, offsets, (tables, weights), emp_own = gather_ring(occ_pair, chips, work, emp_own)
    emp_other = lax.ppermute(emp_own, "space", swap)

    results = []
    own_count = cos_weights.shape[0] // tm
    part_rows = NG // space
    for w in range(own_count):
        keep_far, send_far, keep_near, send_near = pair_moment(
            weights[w], occ_blocks, offsets, emp_own, emp_other, tables
        )
        far_total = keep_far + lax.ppermute(send_far, "space", swap).astype(jnp.float32)
        near_total = keep_near + lax.ppermute(send_near, "space", swap).astype(jnp.float32)
        far = far_slots(chips)
        near = [slot for slot in range(chips) if slot not in far]
        totals = {}
        for slots, total in ((far, far_total), (near, near_total)):
            for index, slot in enumerate(slots):
                start = index * round_up(part_rows, 16)
                totals[slot] = total[start : start + part_rows]
        results.append(reduce_ring(totals, chips))
    return jnp.stack(results)


def solution(mesh):
    return jax.shard_map(
        functools.partial(local, mesh.shape["space"], mesh.shape["tm"]),
        mesh=mesh,
        in_specs=(P("space", None), P(), P("tm"), P()),
        out_specs=P("tm", "space", None),
        check_vma=False,
    )
```

```python
import functools
import math

import jax
import jax.numpy as jnp
from jax import lax
from jax.experimental import pallas as pl
from jax.experimental.pallas import tpu as pltpu
from jax.sharding import PartitionSpec as P

SIDE = 24
NG = 864
NOCC = 64
NEMP = 256
LANES = 128
PLANES = 3


def round_up(value, step):
    return -(-value // step) * step


def pair_weights(tm, own_count, time_count, n_occ, n_emp, place_ref, scalar_ref, out_ref):
    me, tm_index = place_ref[0], place_ref[1]
    core, own_chip = lax.rem(me, 2), lax.div(me, 2)
    shape = out_ref.shape[1:]
    pair = lax.broadcasted_iota(jnp.int32, shape, 0) * LANES + lax.broadcasted_iota(jnp.int32, shape, 1)
    occ_number = lax.rem(pair, n_occ)
    occ_gap = jnp.zeros(shape, jnp.float32)
    emp_gap = jnp.zeros(shape, jnp.float32)
    for i in range(n_occ):
        occ_gap = jnp.where(occ_number == i, scalar_ref[core * n_occ + i], occ_gap)
    for j in range(n_emp):
        emp_gap = jnp.where(pair >= j * n_occ, scalar_ref[NOCC + own_chip * n_emp + j], emp_gap)
    first_time = NOCC + NEMP
    first_share = first_time + time_count
    weights = [jnp.zeros(shape, jnp.float32) for _ in range(own_count)]
    for k in range(time_count):
        hop, number = divmod(k, time_count // tm)
        source = lax.rem(tm_index + hop, tm) * (time_count // tm) + number
        time = scalar_ref[first_time + k]
        occ_factor = jnp.exp(-occ_gap * time) * NOCC ** (-0.5)
        emp_factor = jnp.exp(-emp_gap * time) * NEMP ** (-0.5)
        for w in range(own_count):
            share = scalar_ref[first_share + (tm_index * own_count + w) * time_count + source]
            weights[w] = weights[w] + share * (occ_factor * emp_factor)
    for w in range(own_count):
        out_ref[w] = weights[w]


def table_kernel(out_ref, with_cos, with_sin):
    kind = pl.program_id(0)
    a_odd, b_odd = kind // 2, kind % 2
    half = SIDE // 2
    a_waves, b_waves, c_waves = SIDE // 4, SIDE // 8, NG // (SIDE // 2 * (SIDE // 4) * 2)
    width = out_ref.shape[2]

    def parts(value, size):
        whole = jnp.floor((value + 0.5) * (1.0 / size))
        return whole, value - size * whole

    column = lax.broadcasted_iota(jnp.int32, (SIDE, width), 1).astype(jnp.float32)
    row = lax.broadcasted_iota(jnp.int32, (SIDE, width), 0).astype(jnp.float32)
    a_step, rest = parts(column, 2 * c_waves * b_waves)
    sine, rest = parts(rest, c_waves * b_waves)
    c_step, b_step = parts(rest, b_waves)
    a = 2.0 * a_step + ((a_odd + a_waves) % 2 - a_waves).astype(jnp.float32)
    b = 2.0 * b_step + ((b_odd + b_waves) % 2 - b_waves).astype(jnp.float32)
    c = c_step + 1.0
    unit = 2.0 * math.pi / SIDE
    size = jnp.where(a_step < a_waves, math.sqrt(2.0 / SIDE**3), 0.0)

    def factors(wave):
        angle = parts(wave * row, SIDE)[1] * unit
        return jnp.cos(angle), jnp.sin(angle)

    cos_p, sin_p = factors(a)
    cos_q, sin_q = factors(b)
    cos_s, sin_s = factors(c)
    is_sine = sine > 0.5
    for y in range(half):
        inner_cos = cos_q[y : y + 1] * cos_s - sin_q[y : y + 1] * sin_s
        inner_sin = sin_q[y : y + 1] * cos_s + cos_q[y : y + 1] * sin_s
        rows = slice(y * SIDE, (y + 1) * SIDE)
        with_cos[rows] = jnp.where(is_sine, inner_sin, inner_cos) * size
        with_sin[rows] = jnp.where(is_sine, inner_cos, -inner_sin) * size
    plane = half * SIDE
    depth = round_up(PLANES * plane, LANES)
    for x in range(half):
        start = x // PLANES * depth + x % PLANES * plane
        table = cos_p[x : x + 1] * with_cos[...] + sin_p[x : x + 1] * with_sin[...]
        out_ref[0, start : start + plane] = table.astype(jnp.bfloat16)
    for step in range(half // PLANES):
        out_ref[0, step * depth + PLANES * plane : (step + 1) * depth] = jnp.zeros(
            (depth - PLANES * plane, width), jnp.bfloat16
        )


def prepare_kernel(
    tm, own_count, time_count, n_occ, n_emp, place_ref, scalar_ref, table_ref, weight_ref, with_cos, with_sin
):
    @pl.when(pl.program_id(0) == 0)
    def _():
        pair_weights(tm, own_count, time_count, n_occ, n_emp, place_ref, scalar_ref, weight_ref)

    table_kernel(table_ref, with_cos, with_sin)


def prepare(place, scalars, tm, own_count, time_count, n_occ, n_emp):
    plane = SIDE * SIDE // 2
    depth = SIDE // 2 // PLANES * round_up(PLANES * plane, LANES)
    width = round_up(NG // 4, 2 * LANES)
    weight_shape = (own_count, n_occ * n_emp // LANES, LANES)
    return pl.pallas_call(
        functools.partial(prepare_kernel, tm, own_count, time_count, n_occ, n_emp),
        grid=(4,),
        out_shape=(
            jax.ShapeDtypeStruct((4, depth, width), jnp.bfloat16),
            jax.ShapeDtypeStruct(weight_shape, jnp.float32),
        ),
        in_specs=[pl.BlockSpec(memory_space=pltpu.SMEM)] * 2,
        out_specs=(
            pl.BlockSpec((1, depth, width), lambda k: (k, 0, 0)),
            pl.BlockSpec(weight_shape, lambda k: (0, 0, 0)),
        ),
        scratch_shapes=[pltpu.VMEM((plane, width), jnp.float32), pltpu.VMEM((plane, width), jnp.float32)],
        compiler_params=pltpu.CompilerParams(vmem_limit_bytes=60 * 1024 * 1024),
        cost_estimate=pl.CostEstimate(
            flops=64 * depth * width, bytes_accessed=8 * depth * width, transcendentals=0
        ),
        name="prepare",
    )(place, scalars)


def ring_place(chip, chips):
    return jnp.where(chip % 2 == 0, chip // 2, chips - (chip + 1) // 2)


def ring_chip(place, chips):
    place = lax.rem(place + chips, chips)
    return jnp.where(place < chips // 2, 2 * place, 2 * (chips - place) - 1)


def far_slots(chips):
    return [chips // 2, chips // 2 + 1]


def pair_kernel(offsets, place_ref, weight_ref, emp_own_ref, emp_other_ref, *refs):
    chips, n_emp, n_rows = emp_own_ref.shape
    shards = 2 * chips
    occ_refs, refs = refs[:chips], refs[chips:]
    table_hbm, keep_far, send_far, keep_near, send_near = refs[:5]
    occ_wide, emp_wide, rho, table, table_sem, raw_sem = refs[5:]
    depth = round_up(PLANES * SIDE * SIDE // 2, LANES)
    steps = table.shape[1] // depth
    n_occ = occ_wide.shape[1]
    per_group = chips // steps
    plane = SIDE * SIDE // 2
    half_emp = n_emp // 2
    half_pairs = half_emp * n_occ

    copy = pltpu.make_async_copy(table_hbm, table, table_sem)
    copy.start()

    me = place_ref[0]
    core, own_chip = lax.rem(me, 2), lax.div(me, 2)
    place = ring_place(own_chip, chips)

    def low_and_high(raw, rows, target):
        for far in range(2):
            for step in range(steps):
                group = far * steps + step
                shard_rows = [
                    raw[group * per_group + shard, rows].astype(jnp.float32) for shard in range(per_group)
                ]
                for upper in range(2):
                    pieces = []
                    for x in range(PLANES):
                        start = (2 * x + upper) * plane
                        stop = start + plane
                        while start < stop:
                            shard, offset = divmod(start, n_rows)
                            count = min(stop - start, n_rows - offset)
                            pieces.append(shard_rows[shard][:, offset : offset + count])
                            start += count
                    pieces.append(jnp.zeros((pieces[0].shape[0], depth - PLANES * plane), jnp.float32))
                    lanes = slice(step * depth, (step + 1) * depth)
                    target[2 * far + upper, rows, lanes] = jnp.concatenate(pieces, axis=1).astype(target.dtype)

    def arrange(raw_occ, raw_emp):
        copies = []
        for index, (offset, ref) in enumerate(zip(offsets, occ_refs, strict=True)):
            chip = ring_chip(place + offset, chips)
            copies += [
                pltpu.make_async_copy(ref.at[0], raw_occ.at[chip * 2 + core], raw_sem.at[4 * index]),
                pltpu.make_async_copy(ref.at[1], raw_occ.at[chip * 2 + 1 - core], raw_sem.at[4 * index + 1]),
                pltpu.make_async_copy(
                    emp_own_ref.at[index], raw_emp.at[index * 2 + core], raw_sem.at[4 * index + 2]
                ),
                pltpu.make_async_copy(
                    emp_other_ref.at[index], raw_emp.at[index * 2 + 1 - core], raw_sem.at[4 * index + 3]
                ),
            ]
        for raw_copy in copies:
            raw_copy.start()
        for raw_copy in copies:
            raw_copy.wait()

        def sixteen(raw, target):
            def rows(part, carry):
                low_and_high(raw, pl.ds(pl.multiple_of(part * 16, 16), 16), target)
                return carry

            lax.fori_loop(0, raw.shape[1] // 16, rows, 0)

        sixteen(raw_occ, occ_wide)
        sixteen(raw_emp, emp_wide)

    pl.run_scoped(
        arrange,
        pltpu.VMEM((shards, n_occ, n_rows), jnp.bfloat16),
        pltpu.VMEM((shards, n_emp, n_rows), jnp.bfloat16),
    )

    def build(half, target, cut):
        emp_rows = [emp_wide[k, half * half_emp : (half + 1) * half_emp, cut] for k in range(4)]
        for i in range(half_emp):
            emp_row = [
                jnp.broadcast_to(emp_rows[k][i : i + 1], (16, LANES)).astype(jnp.bfloat16) for k in range(4)
            ]
            for part in range(0, n_occ, 16):
                near_low, near_high, far_low, far_high = (
                    emp_row[k] * occ_wide[k, part : part + 16, cut] for k in range(4)
                )
                even_low, odd_low = near_low + far_low, near_low - far_low
                even_high, odd_high = near_high + far_high, near_high - far_high
                rows = slice(i * n_occ + part, i * n_occ + part + 16)
                target[0, rows, cut] = even_low + even_high
                target[1, rows, cut] = even_low - even_high
                target[2, rows, cut] = odd_low + odd_high
                target[3, rows, cut] = odd_low - odd_high

    modes = rho.shape[1]
    spacing = SIDE
    per_a = modes // spacing

    def multiply(half, source, k):
        found = jnp.dot(source[k], table[k], preferred_element_type=jnp.float32).T
        a_odd, b_odd = divmod(k, 2)
        a_first = (a_odd + SIDE // 4) % 2
        b_first = (b_odd + SIDE // 8) % 2
        for a_step in range(SIDE // 4):
            start = b_first * (SIDE // 2) + 2 * a_step + a_first
            for tile in range(half_pairs // LANES):
                rho[half * half_pairs // LANES + tile, pl.ds(start, per_a, stride=spacing), :] = found[
                    a_step * per_a : (a_step + 1) * per_a, tile * LANES : (tile + 1) * LANES
                ]

    chunks = steps * depth // LANES

    def transform(first, second):
        def build_first(chunk, carry):
            build(0, first, pl.ds(pl.multiple_of(chunk * LANES, LANES), LANES))
            return carry

        lax.fori_loop(0, chunks, build_first, 0)
        copy.wait()
        for k in range(4):
            for chunk in range(k * chunks // 4, (k + 1) * chunks // 4):
                build(1, second, slice(chunk * LANES, (chunk + 1) * LANES))
            multiply(0, first, k)
        for k in range(4):
            multiply(1, second, k)

    product = pltpu.VMEM((4, half_pairs, steps * depth), jnp.bfloat16)
    pl.run_scoped(transform, product, product)

    rows = NG // shards

    def combine(blocks):
        tiles = range(rho.shape[0])
        ordered = jnp.concatenate([rho[tile].astype(jnp.bfloat16) for tile in tiles], axis=1)
        per_part = shards // 4
        for part in range(4):
            cut = slice(part * per_part * rows, (part + 1) * per_part * rows)
            weighted = jnp.concatenate(
                [(rho[tile, cut] * weight_ref[tile : tile + 1]).astype(jnp.bfloat16) for tile in tiles], axis=1
            )
            moment = lax.dot_general(
                weighted, ordered, (((1,), (1,)), ((), ())), preferred_element_type=jnp.float32
            )
            for k in range(per_part):
                blocks[part * per_part + k] = moment[k * rows : (k + 1) * rows]
        far = far_slots(chips)
        near = [slot for slot in range(chips) if slot not in far]
        for slots, keep, send in ((far, keep_far, send_far), (near, keep_near, send_near)):
            for index, slot in enumerate(slots):
                chip = ring_chip(place + slot, chips)
                start = index * round_up(rows, 16)
                keep[start : start + rows, :NG] = blocks[2 * chip + core]
                send[start : start + rows, :NG] = blocks[2 * chip + 1 - core].astype(jnp.bfloat16)

    pl.run_scoped(combine, pltpu.VMEM((shards, rows, NG), jnp.float32))


def pair_moment(place, weights, occ_blocks, offsets, emp_own, emp_other, tables):
    chips, n_emp, _ = emp_own.shape
    n_occ = occ_blocks[0].shape[1]
    _, depth, width = tables.shape
    pairs = n_occ * n_emp
    rows = NG // (2 * chips)
    far_rows, near_rows = 2 * round_up(rows, 16), (chips - 2) * round_up(rows, 16)
    smem = pl.BlockSpec(memory_space=pltpu.SMEM)
    vmem = pl.BlockSpec(memory_space=pltpu.VMEM)
    hbm = pl.BlockSpec(memory_space=pl.ANY)
    return pl.pallas_call(
        functools.partial(pair_kernel, offsets),
        out_shape=tuple(
            jax.ShapeDtypeStruct((count, round_up(NG, LANES)), dtype)
            for count in (far_rows, near_rows)
            for dtype in (jnp.float32, jnp.bfloat16)
        ),
        in_specs=[smem, vmem] + [hbm] * (chips + 3),
        out_specs=(vmem, vmem, vmem, vmem),
        scratch_shapes=[
            pltpu.VMEM((4, n_occ, depth), jnp.bfloat16),
            pltpu.VMEM((4, n_emp, depth), jnp.float32),
            pltpu.VMEM((pairs // LANES, NG, LANES), jnp.float32),
            pltpu.VMEM((4, depth, width), jnp.bfloat16),
            pltpu.SemaphoreType.DMA,
            pltpu.SemaphoreType.DMA((4 * chips,)),
        ],
        compiler_params=pltpu.CompilerParams(vmem_limit_bytes=60 * 1024 * 1024),
        cost_estimate=pl.CostEstimate(
            flops=8 * pairs * depth * width, bytes_accessed=16 * 2**20, transcendentals=0
        ),
        name="pair_moment",
    )(place, weights, emp_own, emp_other, *occ_blocks, tables)


def ring_steps(chips):
    ring = list(range(0, chips, 2)) + list(range(chips - 1, 0, -2))
    ahead = [
        (2 * ring[k] + core, 2 * ring[(k + 1) % chips] + core) for k in range(chips) for core in range(2)
    ]
    return ahead, [(to, start) for start, to in ahead]


def hold(value, until):
    return lax.optimization_barrier((value, until))[0]


def gather_ring(block, chips, second, third):
    ahead, back = ring_steps(chips)
    found, offsets = [block], [0]
    from_left = from_right = block
    for hop in range(1, chips // 2 + 1):
        if hop == 2:
            from_left, from_right, second = lax.optimization_barrier((from_left, from_right, second))
        elif hop == 3:
            from_left, from_right, third = lax.optimization_barrier((from_left, from_right, third))
        elif hop > 3:
            from_left, from_right = lax.optimization_barrier((from_left, from_right))
        from_left = lax.ppermute(from_left, "space", ahead)
        found.append(from_left)
        offsets.append(-hop)
        if 2 * hop < chips:
            from_right = lax.ppermute(from_right, "space", back)
            found.append(from_right)
            offsets.append(hop)
    return found, offsets, second, third


def reduce_ring(totals, chips):
    ahead, back = ring_steps(chips)
    farthest = chips // 2
    from_left, from_right = totals[farthest], totals[farthest + 1]
    for hop in range(1, farthest + 1):
        from_left = lax.ppermute(from_left.astype(jnp.bfloat16), "space", ahead).astype(jnp.float32)
        if hop < farthest:
            from_right = lax.ppermute(from_right.astype(jnp.bfloat16), "space", back).astype(jnp.float32)
            from_left = from_left + totals[farthest - hop]
        if hop < farthest - 1:
            from_right = from_right + totals[farthest + 1 + hop]
    return (totals[0] + from_left + from_right)[:, :NG]


def local(space, tm, orbitals, gaps, times, cos_weights):
    rows = orbitals.shape[0]
    chips = space // 2
    columns = orbitals.T
    own_occ, own_emp = NOCC // 2, NEMP // chips
    own_count, time_count = cos_weights.shape[0] // tm, cos_weights.shape[1]
    me = lax.axis_index("space")
    core = me % 2
    swap = [(d, d ^ 1) for d in range(space)]

    every_time = [times] + [
        lax.ppermute(times, "tm", [((d + hop) % tm, d) for d in range(tm)]) for hop in range(1, tm)
    ]
    scalars = jnp.concatenate([gaps] + every_time + [cos_weights.reshape(-1)])
    place = jnp.stack([me, lax.axis_index("tm")]).astype(jnp.int32)

    occ = columns[:NOCC].reshape(2, own_occ, rows)
    occ_mine = lax.dynamic_index_in_dim(occ, core, 0, keepdims=False)
    occ_theirs = lax.dynamic_index_in_dim(occ, 1 - core, 0, keepdims=False)
    occ_pair = jnp.stack([occ_mine, lax.ppermute(occ_theirs, "space", swap)])
    emp_own = lax.all_to_all(
        columns[NOCC:].reshape(chips, own_emp, rows),
        "space",
        split_axis=0,
        concat_axis=0,
        axis_index_groups=[[2 * k + c for k in range(chips)] for c in range(2)],
    )
    made = prepare(place, hold(scalars, occ_pair), tm, own_count, time_count, own_occ, own_emp)
    occ_blocks, offsets, (tables, weights), emp_own = gather_ring(occ_pair, chips, made, emp_own)
    emp_other = lax.ppermute(emp_own, "space", swap)

    results = []
    part_rows = NG // space
    for w in range(own_count):
        keep_far, send_far, keep_near, send_near = pair_moment(
            place, weights[w], occ_blocks, offsets, emp_own, emp_other, tables
        )
        far_total = keep_far + lax.ppermute(send_far, "space", swap).astype(jnp.float32)
        near_total = keep_near + lax.ppermute(send_near, "space", swap).astype(jnp.float32)
        far = far_slots(chips)
        near = [slot for slot in range(chips) if slot not in far]
        totals = {}
        for slots, total in ((far, far_total), (near, near_total)):
            for index, slot in enumerate(slots):
                start = index * round_up(part_rows, 16)
                totals[slot] = total[start : start + part_rows]
        results.append(reduce_ring(totals, chips))
    return jnp.stack(results)


def solution(mesh):
    return jax.shard_map(
        functools.partial(local, mesh.shape["space"], mesh.shape["tm"]),
        mesh=mesh,
        in_specs=(P("space", None), P(), P("tm"), P()),
        out_specs=P("tm", "space", None),
        check_vma=False,
    )
```

```python
import functools
import math

import jax
import jax.numpy as jnp
from jax import lax
from jax.experimental import pallas as pl
from jax.experimental.pallas import tpu as pltpu
from jax.sharding import PartitionSpec as P

SIDE = 24
NG = 864
NOCC = 64
NEMP = 256
LANES = 128
PLANES = 3


def round_up(value, step):
    return -(-value // step) * step


def pair_weights(tm, own_count, time_count, n_occ, n_emp, place_ref, scalar_ref, out_ref):
    me, tm_index = place_ref[0], place_ref[1]
    core, own_chip = lax.rem(me, 2), lax.div(me, 2)
    shape = out_ref.shape[1:]
    pair = lax.broadcasted_iota(jnp.int32, shape, 0) * LANES + lax.broadcasted_iota(jnp.int32, shape, 1)
    occ_number = lax.rem(pair, n_occ)
    occ_gap = jnp.zeros(shape, jnp.float32)
    emp_gap = jnp.zeros(shape, jnp.float32)
    for i in range(n_occ):
        occ_gap = jnp.where(occ_number == i, scalar_ref[core * n_occ + i], occ_gap)
    for j in range(n_emp):
        emp_gap = jnp.where(pair >= j * n_occ, scalar_ref[NOCC + own_chip * n_emp + j], emp_gap)
    first_time = NOCC + NEMP
    first_share = first_time + time_count
    weights = [jnp.zeros(shape, jnp.float32) for _ in range(own_count)]
    for k in range(time_count):
        hop, number = divmod(k, time_count // tm)
        source = lax.rem(tm_index + hop, tm) * (time_count // tm) + number
        time = scalar_ref[first_time + k]
        occ_factor = jnp.exp(-occ_gap * time) * NOCC ** (-0.5)
        emp_factor = jnp.exp(-emp_gap * time) * NEMP ** (-0.5)
        for w in range(own_count):
            share = scalar_ref[first_share + (tm_index * own_count + w) * time_count + source]
            weights[w] = weights[w] + share * (occ_factor * emp_factor)
    for w in range(own_count):
        out_ref[w] = weights[w]


def table_kernel(held_ref, out_ref, with_cos, with_sin):
    kind = pl.program_id(0) + held_ref[0]
    a_odd, b_odd = kind // 2, kind % 2
    half = SIDE // 2
    a_waves, b_waves, c_waves = SIDE // 4, SIDE // 8, NG // (SIDE // 2 * (SIDE // 4) * 2)
    width = out_ref.shape[2]

    def parts(value, size):
        whole = jnp.floor((value + 0.5) * (1.0 / size))
        return whole, value - size * whole

    column = lax.broadcasted_iota(jnp.int32, (SIDE, width), 1).astype(jnp.float32)
    row = lax.broadcasted_iota(jnp.int32, (SIDE, width), 0).astype(jnp.float32)
    a_step, rest = parts(column, 2 * c_waves * b_waves)
    sine, rest = parts(rest, c_waves * b_waves)
    c_step, b_step = parts(rest, b_waves)
    a = 2.0 * a_step + ((a_odd + a_waves) % 2 - a_waves).astype(jnp.float32)
    b = 2.0 * b_step + ((b_odd + b_waves) % 2 - b_waves).astype(jnp.float32)
    c = c_step + 1.0
    unit = 2.0 * math.pi / SIDE
    size = jnp.where(a_step < a_waves, math.sqrt(2.0 / SIDE**3), 0.0)

    def factors(wave):
        angle = parts(wave * row, SIDE)[1] * unit
        return jnp.cos(angle), jnp.sin(angle)

    cos_p, sin_p = factors(a)
    cos_q, sin_q = factors(b)
    cos_s, sin_s = factors(c)
    is_sine = sine > 0.5
    for y in range(half):
        inner_cos = cos_q[y : y + 1] * cos_s - sin_q[y : y + 1] * sin_s
        inner_sin = sin_q[y : y + 1] * cos_s + cos_q[y : y + 1] * sin_s
        rows = slice(y * SIDE, (y + 1) * SIDE)
        with_cos[rows] = jnp.where(is_sine, inner_sin, inner_cos) * size
        with_sin[rows] = jnp.where(is_sine, inner_cos, -inner_sin) * size
    plane = half * SIDE
    depth = round_up(PLANES * plane, LANES)
    for x in range(half):
        start = x // PLANES * depth + x % PLANES * plane
        table = cos_p[x : x + 1] * with_cos[...] + sin_p[x : x + 1] * with_sin[...]
        out_ref[0, start : start + plane] = table.astype(jnp.bfloat16)
    for step in range(half // PLANES):
        out_ref[0, step * depth + PLANES * plane : (step + 1) * depth] = jnp.zeros(
            (depth - PLANES * plane, width), jnp.bfloat16
        )


def class_tables(held):
    plane = SIDE * SIDE // 2
    depth = SIDE // 2 // PLANES * round_up(PLANES * plane, LANES)
    width = round_up(NG // 4, 2 * LANES)
    return pl.pallas_call(
        table_kernel,
        grid=(4,),
        out_shape=jax.ShapeDtypeStruct((4, depth, width), jnp.bfloat16),
        in_specs=[pl.BlockSpec(memory_space=pltpu.SMEM)],
        out_specs=pl.BlockSpec((1, depth, width), lambda k: (k, 0, 0)),
        scratch_shapes=[pltpu.VMEM((plane, width), jnp.float32), pltpu.VMEM((plane, width), jnp.float32)],
        compiler_params=pltpu.CompilerParams(vmem_limit_bytes=60 * 1024 * 1024),
        cost_estimate=pl.CostEstimate(
            flops=64 * depth * width, bytes_accessed=8 * depth * width, transcendentals=0
        ),
        name="class_tables",
    )(held)


def all_pair_weights(place, scalars, tm, own_count, time_count, n_occ, n_emp):
    smem = pl.BlockSpec(memory_space=pltpu.SMEM)
    return pl.pallas_call(
        functools.partial(pair_weights, tm, own_count, time_count, n_occ, n_emp),
        out_shape=jax.ShapeDtypeStruct((own_count, n_occ * n_emp // LANES, LANES), jnp.float32),
        in_specs=[smem, smem],
        out_specs=pl.BlockSpec(memory_space=pltpu.VMEM),
        cost_estimate=pl.CostEstimate(flops=2**24, bytes_accessed=2**20, transcendentals=0),
        name="pair_weights",
    )(place, scalars)


def ring_place(chip, chips):
    return jnp.where(chip % 2 == 0, chip // 2, chips - (chip + 1) // 2)


def ring_chip(place, chips):
    place = lax.rem(place + chips, chips)
    return jnp.where(place < chips // 2, 2 * place, 2 * (chips - place) - 1)


def far_slots(chips):
    return [chips // 2, chips // 2 + 1]


def pair_kernel(offsets, splits, place_ref, weight_ref, *refs):
    emp_refs, refs = refs[: 2 * splits], refs[2 * splits :]
    chips, part_emp, n_rows = emp_refs[0].shape
    n_emp = splits * part_emp
    shards = 2 * chips
    occ_refs, refs = refs[:chips], refs[chips:]
    table_hbm, keep_far, send_far, keep_near, send_near = refs[:5]
    occ_wide, emp_wide, rho, table, table_sem, raw_sem = refs[5:]
    depth = round_up(PLANES * SIDE * SIDE // 2, LANES)
    steps = table.shape[1] // depth
    n_occ = occ_wide.shape[1]
    per_group = chips // steps
    plane = SIDE * SIDE // 2
    half_emp = n_emp // 2
    half_pairs = half_emp * n_occ

    copy = pltpu.make_async_copy(table_hbm, table, table_sem)
    me = place_ref[0]
    core, own_chip = lax.rem(me, 2), lax.div(me, 2)
    place = ring_place(own_chip, chips)

    def low_and_high(raw, rows, target):
        for far in range(2):
            for step in range(steps):
                group = far * steps + step
                first_chip = group * per_group // 2
                shard_rows = [
                    raw[first_chip + shard // 2, shard % 2, rows].astype(jnp.float32)
                    for shard in range(per_group)
                ]
                for upper in range(2):
                    pieces = []
                    for x in range(PLANES):
                        start = (2 * x + upper) * plane
                        stop = start + plane
                        while start < stop:
                            shard, offset = divmod(start, n_rows)
                            count = min(stop - start, n_rows - offset)
                            pieces.append(shard_rows[shard][:, offset : offset + count])
                            start += count
                    pieces.append(jnp.zeros((pieces[0].shape[0], depth - PLANES * plane), jnp.float32))
                    lanes = slice(step * depth, (step + 1) * depth)
                    target[2 * far + upper, rows, lanes] = jnp.concatenate(pieces, axis=1).astype(target.dtype)

    def arrange(raw_occ, raw_emp):
        copies = []
        for index, (offset, ref) in enumerate(zip(offsets, occ_refs, strict=True)):
            chip = ring_chip(place + offset, chips)
            for other in range(2):
                target = raw_occ.at[chip, 1 - core if other else core]
                copies.append(pltpu.make_async_copy(ref.at[other], target, raw_sem.at[2 * index + other]))
        for index, ref in enumerate(emp_refs):
            part, other = divmod(index, 2)
            start = pl.multiple_of(lax.rem(place_ref[1] + part, splits) * part_emp, part_emp)
            target = raw_emp.at[:, 1 - core if other else core, pl.ds(start, part_emp)]
            copies.append(pltpu.make_async_copy(ref, target, raw_sem.at[shards + index]))
        for raw_copy in copies:
            raw_copy.start()
        for raw_copy in copies:
            raw_copy.wait()
        copy.start()

        def sixteen(raw, target):
            def rows(part, carry):
                low_and_high(raw, pl.ds(pl.multiple_of(part * 16, 16), 16), target)
                return carry

            lax.fori_loop(0, raw.shape[2] // 16, rows, 0)

        sixteen(raw_occ, occ_wide)
        sixteen(raw_emp, emp_wide)

    pl.run_scoped(
        arrange,
        pltpu.VMEM((chips, 2, n_occ, n_rows), jnp.bfloat16),
        pltpu.VMEM((chips, 2, n_emp, n_rows), jnp.bfloat16),
    )

    def build(half, target, cut):
        emp_rows = [emp_wide[k, half * half_emp : (half + 1) * half_emp, cut] for k in range(4)]
        for i in range(half_emp):
            emp_row = [
                jnp.broadcast_to(emp_rows[k][i : i + 1], (16, LANES)).astype(jnp.bfloat16) for k in range(4)
            ]
            for part in range(0, n_occ, 16):
                near_low, near_high, far_low, far_high = (
                    emp_row[k] * occ_wide[k, part : part + 16, cut] for k in range(4)
                )
                even_low, odd_low = near_low + far_low, near_low - far_low
                even_high, odd_high = near_high + far_high, near_high - far_high
                rows = slice(i * n_occ + part, i * n_occ + part + 16)
                target[0, rows, cut] = even_low + even_high
                target[1, rows, cut] = even_low - even_high
                target[2, rows, cut] = odd_low + odd_high
                target[3, rows, cut] = odd_low - odd_high

    modes = rho.shape[1]
    spacing = SIDE
    per_a = modes // spacing

    def multiply(half, source, k):
        found = jnp.dot(source[k], table[k], preferred_element_type=jnp.float32).T
        a_odd, b_odd = divmod(k, 2)
        a_first = (a_odd + SIDE // 4) % 2
        b_first = (b_odd + SIDE // 8) % 2
        for a_step in range(SIDE // 4):
            start = b_first * (SIDE // 2) + 2 * a_step + a_first
            for tile in range(half_pairs // LANES):
                rho[half * half_pairs // LANES + tile, pl.ds(start, per_a, stride=spacing), :] = found[
                    a_step * per_a : (a_step + 1) * per_a, tile * LANES : (tile + 1) * LANES
                ]

    chunks = steps * depth // LANES

    def transform(first, second):
        def build_first(chunk, carry):
            build(0, first, pl.ds(pl.multiple_of(chunk * LANES, LANES), LANES))
            return carry

        lax.fori_loop(0, chunks, build_first, 0)
        copy.wait()
        for k in range(4):
            for chunk in range(k * chunks // 4, (k + 1) * chunks // 4):
                build(1, second, slice(chunk * LANES, (chunk + 1) * LANES))
            multiply(0, first, k)
        for k in range(4):
            multiply(1, second, k)

    product = pltpu.VMEM((4, half_pairs, steps * depth), jnp.bfloat16)
    pl.run_scoped(transform, product, product)

    rows = NG // shards

    def combine(blocks):
        tiles = range(rho.shape[0])
        ordered = jnp.concatenate([rho[tile].astype(jnp.bfloat16) for tile in tiles], axis=1)
        weighted = jnp.concatenate(
            [(rho[tile] * weight_ref[tile : tile + 1]).astype(jnp.bfloat16) for tile in tiles], axis=1
        )
        moment = lax.dot_general(
            weighted, ordered, (((1,), (1,)), ((), ())), preferred_element_type=jnp.float32
        )
        for k in range(shards):
            blocks[k] = moment[k * rows : (k + 1) * rows]
        far = far_slots(chips)
        near = [slot for slot in range(chips) if slot not in far]
        for slots, keep, send in ((far, keep_far, send_far), (near, keep_near, send_near)):
            for index, slot in enumerate(slots):
                chip = ring_chip(place + slot, chips)
                start = index * round_up(rows, 16)
                keep[start : start + rows, :NG] = blocks[2 * chip + core]
                send[start : start + rows, :NG] = blocks[2 * chip + 1 - core].astype(jnp.bfloat16)

    pl.run_scoped(combine, pltpu.VMEM((shards, rows, NG), jnp.float32))


def pair_moment(place, weights, occ_blocks, offsets, emp_parts, tables):
    splits = len(emp_parts) // 2
    chips, part_emp, _ = emp_parts[0].shape
    n_emp = splits * part_emp
    n_occ = occ_blocks[0].shape[1]
    _, depth, width = tables.shape
    pairs = n_occ * n_emp
    rows = NG // (2 * chips)
    far_rows, near_rows = 2 * round_up(rows, 16), (chips - 2) * round_up(rows, 16)
    smem = pl.BlockSpec(memory_space=pltpu.SMEM)
    vmem = pl.BlockSpec(memory_space=pltpu.VMEM)
    hbm = pl.BlockSpec(memory_space=pl.ANY)
    return pl.pallas_call(
        functools.partial(pair_kernel, offsets, splits),
        out_shape=tuple(
            jax.ShapeDtypeStruct((count, round_up(NG, LANES)), dtype)
            for count in (far_rows, near_rows)
            for dtype in (jnp.float32, jnp.bfloat16)
        ),
        in_specs=[smem, vmem] + [hbm] * (2 * splits + chips + 1),
        out_specs=(vmem, vmem, vmem, vmem),
        scratch_shapes=[
            pltpu.VMEM((4, n_occ, depth), jnp.bfloat16),
            pltpu.VMEM((4, n_emp, depth), jnp.float32),
            pltpu.VMEM((pairs // LANES, NG, LANES), jnp.float32),
            pltpu.VMEM((4, depth, width), jnp.bfloat16),
            pltpu.SemaphoreType.DMA,
            pltpu.SemaphoreType.DMA((2 * chips + 2 * splits,)),
        ],
        compiler_params=pltpu.CompilerParams(vmem_limit_bytes=60 * 1024 * 1024),
        cost_estimate=pl.CostEstimate(
            flops=8 * pairs * depth * width, bytes_accessed=16 * 2**20, transcendentals=0
        ),
        name="pair_moment",
    )(place, weights, *emp_parts, *occ_blocks, tables)


def ring_steps(chips):
    ring = list(range(0, chips, 2)) + list(range(chips - 1, 0, -2))
    ahead = [
        (2 * ring[k] + core, 2 * ring[(k + 1) % chips] + core) for k in range(chips) for core in range(2)
    ]
    return ahead, [(to, start) for start, to in ahead]


def hold(value, until):
    return lax.optimization_barrier((value, until))[0]


def reduce_ring(totals, chips):
    ahead, back = ring_steps(chips)
    farthest = chips // 2
    from_left, from_right = totals[farthest], totals[farthest + 1]
    for hop in range(1, farthest + 1):
        from_left = lax.ppermute(from_left.astype(jnp.bfloat16), "space", ahead).astype(jnp.float32)
        if hop < farthest:
            from_right = lax.ppermute(from_right.astype(jnp.bfloat16), "space", back).astype(jnp.float32)
            from_left = from_left + totals[farthest - hop]
        if hop < farthest - 1:
            from_right = from_right + totals[farthest + 1 + hop]
    return (totals[0] + from_left + from_right)[:, :NG]


def local(space, tm, orbitals, gaps, times, cos_weights):
    rows = orbitals.shape[0]
    chips = space // 2
    columns = orbitals.T
    own_occ, own_emp = NOCC // 2, NEMP // chips
    own_count, time_count = cos_weights.shape[0] // tm, cos_weights.shape[1]
    me = lax.axis_index("space")
    core = me % 2
    swap = [(d, d ^ 1) for d in range(space)]

    every_time = [times] + [
        lax.ppermute(times, "tm", [((d + hop) % tm, d) for d in range(tm)]) for hop in range(1, tm)
    ]
    scalars = jnp.concatenate([gaps] + every_time + [cos_weights.reshape(-1)])
    place = jnp.stack([me, lax.axis_index("tm")]).astype(jnp.int32)

    occ = columns[:NOCC].reshape(2, own_occ, rows)
    occ_mine = lax.dynamic_index_in_dim(occ, core, 0, keepdims=False)
    occ_theirs = lax.dynamic_index_in_dim(occ, 1 - core, 0, keepdims=False)
    occ_pair = jnp.stack([occ_mine, lax.ppermute(occ_theirs, "space", swap)])
    splits = tm if tm == 2 else 1
    emp_columns = lax.dynamic_slice(
        columns.reshape((NOCC + NEMP) // own_emp, splits, own_emp // splits, rows),
        (NOCC // own_emp, lax.axis_index("tm") % splits, 0, 0),
        (chips, 1, own_emp // splits, rows),
    )
    emp = lax.all_to_all(
        emp_columns.reshape(chips, own_emp // splits, rows),
        "space",
        split_axis=0,
        concat_axis=0,
        axis_index_groups=[[2 * k + c for k in range(chips)] for c in range(2)],
    )

    tables = class_tables(hold(jnp.zeros((1,), jnp.int32), occ_pair))
    emp_parts = []
    ahead, back = ring_steps(chips)
    found, offsets = [occ_pair], [0]
    from_left = from_right = occ_pair
    for hop in range(1, chips // 2 + 1):
        if hop == 2:
            from_left, from_right, emp, tables = lax.optimization_barrier((from_left, from_right, emp, tables))
            emp_parts += [emp, lax.ppermute(emp, "space", swap)]
            traded = lax.ppermute(emp, "tm", [(0, 1), (1, 0)]) if splits > 1 else None
        elif hop == 3:
            from_left, from_right, traded = lax.optimization_barrier((from_left, from_right, traded))
            if splits > 1:
                emp_parts += [traded, lax.ppermute(traded, "space", swap)]
            weights = all_pair_weights(
                place, hold(scalars, (from_left, from_right)), tm, own_count, time_count, own_occ, own_emp
            )
        elif hop == 4:
            from_left, from_right, weights = lax.optimization_barrier((from_left, from_right, weights))
        elif hop > 4:
            from_left, from_right = lax.optimization_barrier((from_left, from_right))
        from_left = lax.ppermute(from_left, "space", ahead)
        found.append(from_left)
        offsets.append(-hop)
        if 2 * hop < chips:
            from_right = lax.ppermute(from_right, "space", back)
            found.append(from_right)
            offsets.append(hop)

    results = []
    part_rows = NG // space
    for w in range(own_count):
        keep_far, send_far, keep_near, send_near = pair_moment(
            place, weights[w], found, offsets, emp_parts, tables
        )
        far_total = keep_far + lax.ppermute(send_far, "space", swap).astype(jnp.float32)
        near_total = keep_near + lax.ppermute(send_near, "space", swap).astype(jnp.float32)
        far = far_slots(chips)
        near = [slot for slot in range(chips) if slot not in far]
        totals = {}
        for slots, total in ((far, far_total), (near, near_total)):
            for index, slot in enumerate(slots):
                start = index * round_up(part_rows, 16)
                totals[slot] = total[start : start + part_rows]
        results.append(reduce_ring(totals, chips))
    return jnp.stack(results)


def solution(mesh):
    return jax.shard_map(
        functools.partial(local, mesh.shape["space"], mesh.shape["tm"]),
        mesh=mesh,
        in_specs=(P("space", None), P(), P("tm"), P()),
        out_specs=P("tm", "space", None),
        check_vma=False,
    )
```

```python
import functools
import math

import jax
import jax.numpy as jnp
from jax import lax
from jax.experimental import pallas as pl
from jax.experimental.pallas import tpu as pltpu
from jax.sharding import PartitionSpec as P

SIDE = 24
NG = 864
NOCC = 64
NEMP = 256
LANES = 128
PLANES = 3


def round_up(value, step):
    return -(-value // step) * step


def pair_weights(tm, own_count, time_count, n_occ, n_emp, place_ref, scalar_ref, out_ref):
    me, tm_index = place_ref[0], place_ref[1]
    core, own_chip = lax.rem(me, 2), lax.div(me, 2)
    shape = out_ref.shape[1:]
    pair = lax.broadcasted_iota(jnp.int32, shape, 0) * LANES + lax.broadcasted_iota(jnp.int32, shape, 1)
    occ_number = lax.rem(pair, n_occ)
    occ_gap = jnp.zeros(shape, jnp.float32)
    emp_gap = jnp.zeros(shape, jnp.float32)
    for i in range(n_occ):
        occ_gap = jnp.where(occ_number == i, scalar_ref[core * n_occ + i], occ_gap)
    for j in range(n_emp):
        emp_gap = jnp.where(pair >= j * n_occ, scalar_ref[NOCC + own_chip * n_emp + j], emp_gap)
    first_time = NOCC + NEMP
    first_share = first_time + time_count
    weights = [jnp.zeros(shape, jnp.float32) for _ in range(own_count)]
    for k in range(time_count):
        hop, number = divmod(k, time_count // tm)
        source = lax.rem(tm_index + hop, tm) * (time_count // tm) + number
        time = scalar_ref[first_time + k]
        occ_factor = jnp.exp(-occ_gap * time) * NOCC ** (-0.5)
        emp_factor = jnp.exp(-emp_gap * time) * NEMP ** (-0.5)
        for w in range(own_count):
            share = scalar_ref[first_share + (tm_index * own_count + w) * time_count + source]
            weights[w] = weights[w] + share * (occ_factor * emp_factor)
    for w in range(own_count):
        out_ref[w] = weights[w]


def table_kernel(held_ref, out_ref, with_cos, with_sin):
    kind = pl.program_id(0) + held_ref[0]
    a_odd, b_odd = kind // 2, kind % 2
    half = SIDE // 2
    a_waves, b_waves, c_waves = SIDE // 4, SIDE // 8, NG // (SIDE // 2 * (SIDE // 4) * 2)
    width = out_ref.shape[2]

    def parts(value, size):
        whole = jnp.floor((value + 0.5) * (1.0 / size))
        return whole, value - size * whole

    column = lax.broadcasted_iota(jnp.int32, (SIDE, width), 1).astype(jnp.float32)
    row = lax.broadcasted_iota(jnp.int32, (SIDE, width), 0).astype(jnp.float32)
    a_step, rest = parts(column, 2 * c_waves * b_waves)
    sine, rest = parts(rest, c_waves * b_waves)
    c_step, b_step = parts(rest, b_waves)
    a = 2.0 * a_step + ((a_odd + a_waves) % 2 - a_waves).astype(jnp.float32)
    b = 2.0 * b_step + ((b_odd + b_waves) % 2 - b_waves).astype(jnp.float32)
    c = c_step + 1.0
    unit = 2.0 * math.pi / SIDE
    size = jnp.where(a_step < a_waves, math.sqrt(2.0 / SIDE**3), 0.0)

    def factors(wave):
        angle = parts(wave * row, SIDE)[1] * unit
        return jnp.cos(angle), jnp.sin(angle)

    cos_p, sin_p = factors(a)
    cos_q, sin_q = factors(b)
    cos_s, sin_s = factors(c)
    is_sine = sine > 0.5
    for y in range(half):
        inner_cos = cos_q[y : y + 1] * cos_s - sin_q[y : y + 1] * sin_s
        inner_sin = sin_q[y : y + 1] * cos_s + cos_q[y : y + 1] * sin_s
        rows = slice(y * SIDE, (y + 1) * SIDE)
        with_cos[rows] = jnp.where(is_sine, inner_sin, inner_cos) * size
        with_sin[rows] = jnp.where(is_sine, inner_cos, -inner_sin) * size
    plane = half * SIDE
    depth = round_up(PLANES * plane, LANES)
    for x in range(half):
        start = x // PLANES * depth + x % PLANES * plane
        table = cos_p[x : x + 1] * with_cos[...] + sin_p[x : x + 1] * with_sin[...]
        out_ref[0, start : start + plane] = table.astype(jnp.bfloat16)
    for step in range(half // PLANES):
        out_ref[0, step * depth + PLANES * plane : (step + 1) * depth] = jnp.zeros(
            (depth - PLANES * plane, width), jnp.bfloat16
        )


def class_tables(held):
    plane = SIDE * SIDE // 2
    depth = SIDE // 2 // PLANES * round_up(PLANES * plane, LANES)
    width = round_up(NG // 4, 2 * LANES)
    return pl.pallas_call(
        table_kernel,
        grid=(4,),
        out_shape=jax.ShapeDtypeStruct((4, depth, width), jnp.bfloat16),
        in_specs=[pl.BlockSpec(memory_space=pltpu.SMEM)],
        out_specs=pl.BlockSpec((1, depth, width), lambda k: (k, 0, 0)),
        scratch_shapes=[pltpu.VMEM((plane, width), jnp.float32), pltpu.VMEM((plane, width), jnp.float32)],
        compiler_params=pltpu.CompilerParams(vmem_limit_bytes=60 * 1024 * 1024),
        cost_estimate=pl.CostEstimate(
            flops=64 * depth * width, bytes_accessed=8 * depth * width, transcendentals=0
        ),
        name="class_tables",
    )(held)


def all_pair_weights(place, scalars, tm, own_count, time_count, n_occ, n_emp):
    smem = pl.BlockSpec(memory_space=pltpu.SMEM)
    return pl.pallas_call(
        functools.partial(pair_weights, tm, own_count, time_count, n_occ, n_emp),
        out_shape=jax.ShapeDtypeStruct((own_count, n_occ * n_emp // LANES, LANES), jnp.float32),
        in_specs=[smem, smem],
        out_specs=pl.BlockSpec(memory_space=pltpu.VMEM),
        cost_estimate=pl.CostEstimate(flops=2**24, bytes_accessed=2**20, transcendentals=0),
        name="pair_weights",
    )(place, scalars)


def ring_place(chip, chips):
    return jnp.where(chip % 2 == 0, chip // 2, chips - (chip + 1) // 2)


def ring_chip(place, chips):
    place = lax.rem(place + chips, chips)
    return jnp.where(place < chips // 2, 2 * place, 2 * (chips - place) - 1)


def far_slots(chips):
    return [chips // 2, chips // 2 + 1]


def pair_kernel(offsets, splits, place_ref, weight_ref, *refs):
    emp_refs, refs = refs[: 2 * splits], refs[2 * splits :]
    chips, part_emp, n_rows = emp_refs[0].shape
    n_emp = splits * part_emp
    shards = 2 * chips
    occ_refs, refs = refs[:chips], refs[chips:]
    table_hbm, keep_far, send_far, keep_near, send_near = refs[:5]
    occ_wide, emp_wide, rho, table, table_sem, raw_sem = refs[5:]
    depth = round_up(PLANES * SIDE * SIDE // 2, LANES)
    steps = table.shape[1] // depth
    n_occ = occ_wide.shape[1]
    per_group = chips // steps
    plane = SIDE * SIDE // 2
    whole_rows = max(1, LANES // n_occ)
    first_emp = max(1, 3 * n_emp // 8 // whole_rows) * whole_rows
    emp_cuts = (slice(0, first_emp), slice(first_emp, n_emp))

    copy = pltpu.make_async_copy(table_hbm, table, table_sem)
    me = place_ref[0]
    core, own_chip = lax.rem(me, 2), lax.div(me, 2)
    place = ring_place(own_chip, chips)

    def low_and_high(raw, rows, target):
        for far in range(2):
            for step in range(steps):
                group = far * steps + step
                first_chip = group * per_group // 2
                shard_rows = [
                    raw[first_chip + shard // 2, shard % 2, rows] for shard in range(per_group)
                ]
                for upper in range(2):
                    pieces = []
                    for x in range(PLANES):
                        start = (2 * x + upper) * plane
                        stop = start + plane
                        while start < stop:
                            shard, offset = divmod(start, n_rows)
                            count = min(stop - start, n_rows - offset)
                            pieces.append(shard_rows[shard][:, offset : offset + count])
                            start += count
                    pieces.append(jnp.zeros((pieces[0].shape[0], depth - PLANES * plane), raw.dtype))
                    lanes = slice(step * depth, (step + 1) * depth)
                    target[2 * far + upper, rows, lanes] = jnp.concatenate(pieces, axis=1).astype(target.dtype)

    def arrange(raw_occ, raw_emp):
        copies = []
        for index, (offset, ref) in enumerate(zip(offsets, occ_refs, strict=True)):
            chip = ring_chip(place + offset, chips)
            for other in range(2):
                target = raw_occ.at[chip, 1 - core if other else core]
                copies.append(pltpu.make_async_copy(ref.at[other], target, raw_sem.at[2 * index + other]))
        for index, ref in enumerate(emp_refs):
            part, other = divmod(index, 2)
            start = pl.multiple_of(lax.rem(place_ref[1] + part, splits) * part_emp, part_emp)
            target = raw_emp.at[:, 1 - core if other else core, pl.ds(start, part_emp)]
            copies.append(pltpu.make_async_copy(ref, target, raw_sem.at[shards + index]))
        for raw_copy in copies:
            raw_copy.start()
        for raw_copy in copies:
            raw_copy.wait()
        copy.start()

        def sixteen(raw, target):
            def rows(part, carry):
                low_and_high(raw, pl.ds(pl.multiple_of(part * 16, 16), 16), target)
                return carry

            lax.fori_loop(0, raw.shape[2] // 16, rows, 0)

        sixteen(raw_occ, occ_wide)
        sixteen(raw_emp, emp_wide)

    pl.run_scoped(
        arrange,
        pltpu.VMEM((chips, 2, n_occ, n_rows), jnp.bfloat16),
        pltpu.VMEM((chips, 2, n_emp, n_rows), jnp.bfloat16),
    )

    def build(half, target, cut):
        emp_rows = [emp_wide[k, emp_cuts[half], cut] for k in range(4)]
        for i in range(emp_rows[0].shape[0]):
            emp_row = [
                jnp.broadcast_to(emp_rows[k][i : i + 1], (16, LANES)).astype(jnp.bfloat16) for k in range(4)
            ]
            for part in range(0, n_occ, 16):
                near_low, near_high, far_low, far_high = (
                    emp_row[k] * occ_wide[k, part : part + 16, cut] for k in range(4)
                )
                even_low, odd_low = near_low + far_low, near_low - far_low
                even_high, odd_high = near_high + far_high, near_high - far_high
                rows = slice(i * n_occ + part, i * n_occ + part + 16)
                target[0, rows, cut] = even_low + even_high
                target[1, rows, cut] = even_low - even_high
                target[2, rows, cut] = odd_low + odd_high
                target[3, rows, cut] = odd_low - odd_high

    modes = rho.shape[1]
    spacing = SIDE
    per_a = modes // spacing

    def multiply(half, source, k):
        found = jnp.dot(source[k], table[k], preferred_element_type=jnp.float32).T
        a_odd, b_odd = divmod(k, 2)
        a_first = (a_odd + SIDE // 4) % 2
        b_first = (b_odd + SIDE // 8) % 2
        for a_step in range(SIDE // 4):
            start = b_first * (SIDE // 2) + 2 * a_step + a_first
            for tile in range(source.shape[1] // LANES):
                rho[emp_cuts[half].start * n_occ // LANES + tile, pl.ds(start, per_a, stride=spacing), :] = found[
                    a_step * per_a : (a_step + 1) * per_a, tile * LANES : (tile + 1) * LANES
                ]

    chunks = steps * depth // LANES

    def transform(first, second):
        def build_first(chunk, carry):
            build(0, first, pl.ds(pl.multiple_of(chunk * LANES, LANES), LANES))
            return carry

        lax.fori_loop(0, chunks, build_first, 0)
        copy.wait()
        for k in range(4):
            for chunk in range(k * chunks // 4, (k + 1) * chunks // 4):
                build(1, second, slice(chunk * LANES, (chunk + 1) * LANES))
            multiply(0, first, k)
        for k in range(4):
            multiply(1, second, k)

    pl.run_scoped(
        transform,
        *(
            pltpu.VMEM((4, (cut.stop - cut.start) * n_occ, steps * depth), jnp.bfloat16) for cut in emp_cuts
        ),
    )

    rows = NG // shards

    def combine(blocks):
        tiles = range(rho.shape[0])
        ordered = jnp.concatenate([rho[tile].astype(jnp.bfloat16) for tile in tiles], axis=1)
        weighted = jnp.concatenate(
            [(rho[tile] * weight_ref[tile : tile + 1]).astype(jnp.bfloat16) for tile in tiles], axis=1
        )
        moment = lax.dot_general(
            weighted, ordered, (((1,), (1,)), ((), ())), preferred_element_type=jnp.float32
        )
        for k in range(shards):
            blocks[k] = moment[k * rows : (k + 1) * rows]
        far = far_slots(chips)
        near = [slot for slot in range(chips) if slot not in far]
        for slots, keep, send in ((far, keep_far, send_far), (near, keep_near, send_near)):
            for index, slot in enumerate(slots):
                chip = ring_chip(place + slot, chips)
                start = index * round_up(rows, 16)
                keep[start : start + rows, :NG] = blocks[2 * chip + core]
                send[start : start + rows, :NG] = blocks[2 * chip + 1 - core].astype(jnp.bfloat16)

    pl.run_scoped(combine, pltpu.VMEM((shards, rows, NG), jnp.float32))


def pair_moment(place, weights, occ_blocks, offsets, emp_parts, tables):
    splits = len(emp_parts) // 2
    chips, part_emp, _ = emp_parts[0].shape
    n_emp = splits * part_emp
    n_occ = occ_blocks[0].shape[1]
    _, depth, width = tables.shape
    pairs = n_occ * n_emp
    rows = NG // (2 * chips)
    far_rows, near_rows = 2 * round_up(rows, 16), (chips - 2) * round_up(rows, 16)
    smem = pl.BlockSpec(memory_space=pltpu.SMEM)
    vmem = pl.BlockSpec(memory_space=pltpu.VMEM)
    hbm = pl.BlockSpec(memory_space=pl.ANY)
    return pl.pallas_call(
        functools.partial(pair_kernel, offsets, splits),
        out_shape=tuple(
            jax.ShapeDtypeStruct((count, round_up(NG, LANES)), dtype)
            for count in (far_rows, near_rows)
            for dtype in (jnp.float32, jnp.bfloat16)
        ),
        in_specs=[smem, vmem] + [hbm] * (2 * splits + chips + 1),
        out_specs=(vmem, vmem, vmem, vmem),
        scratch_shapes=[
            pltpu.VMEM((4, n_occ, depth), jnp.bfloat16),
            pltpu.VMEM((4, n_emp, depth), jnp.float32),
            pltpu.VMEM((pairs // LANES, NG, LANES), jnp.float32),
            pltpu.VMEM((4, depth, width), jnp.bfloat16),
            pltpu.SemaphoreType.DMA,
            pltpu.SemaphoreType.DMA((2 * chips + 2 * splits,)),
        ],
        compiler_params=pltpu.CompilerParams(vmem_limit_bytes=60 * 1024 * 1024),
        cost_estimate=pl.CostEstimate(
            flops=8 * pairs * depth * width, bytes_accessed=16 * 2**20, transcendentals=0
        ),
        name="pair_moment",
    )(place, weights, *emp_parts, *occ_blocks, tables)


def ring_steps(chips):
    ring = list(range(0, chips, 2)) + list(range(chips - 1, 0, -2))
    ahead = [
        (2 * ring[k] + core, 2 * ring[(k + 1) % chips] + core) for k in range(chips) for core in range(2)
    ]
    return ahead, [(to, start) for start, to in ahead]


def hold(value, until):
    return lax.optimization_barrier((value, until))[0]


def reduce_ring(totals, chips):
    ahead, back = ring_steps(chips)
    farthest = chips // 2
    from_left, from_right = totals[farthest], totals[farthest + 1]
    for hop in range(1, farthest + 1):
        from_left = lax.ppermute(from_left.astype(jnp.bfloat16), "space", ahead).astype(jnp.float32)
        if hop < farthest:
            from_right = lax.ppermute(from_right.astype(jnp.bfloat16), "space", back).astype(jnp.float32)
            from_left = from_left + totals[farthest - hop]
        if hop < farthest - 1:
            from_right = from_right + totals[farthest + 1 + hop]
    return (totals[0] + from_left + from_right)[:, :NG]


def local(space, tm, orbitals, gaps, times, cos_weights):
    rows = orbitals.shape[0]
    chips = space // 2
    columns = orbitals.T
    own_occ, own_emp = NOCC // 2, NEMP // chips
    own_count, time_count = cos_weights.shape[0] // tm, cos_weights.shape[1]
    me = lax.axis_index("space")
    core = me % 2
    swap = [(d, d ^ 1) for d in range(space)]

    place = jnp.stack([me, lax.axis_index("tm")]).astype(jnp.int32)

    occ = columns[:NOCC].reshape(2, own_occ, rows)
    occ_mine = lax.dynamic_index_in_dim(occ, core, 0, keepdims=False)
    occ_theirs = lax.dynamic_index_in_dim(occ, 1 - core, 0, keepdims=False)
    occ_pair = jnp.stack([occ_mine, lax.ppermute(occ_theirs, "space", swap)])
    splits = tm if tm == 2 else 1
    emp_columns = lax.dynamic_slice(
        columns.reshape((NOCC + NEMP) // own_emp, splits, own_emp // splits, rows),
        (NOCC // own_emp, lax.axis_index("tm") % splits, 0, 0),
        (chips, 1, own_emp // splits, rows),
    )
    emp = lax.all_to_all(
        emp_columns.reshape(chips, own_emp // splits, rows),
        "space",
        split_axis=0,
        concat_axis=0,
        axis_index_groups=[[2 * k + c for k in range(chips)] for c in range(2)],
    )

    tables = class_tables(hold(jnp.zeros((1,), jnp.int32), occ_pair))
    emp_parts = []
    ahead, back = ring_steps(chips)
    found, offsets = [occ_pair], [0]
    from_left = from_right = occ_pair
    for hop in range(1, chips // 2 + 1):
        if hop == 2:
            from_left, from_right, emp, tables = lax.optimization_barrier((from_left, from_right, emp, tables))
            emp_parts += [emp, lax.ppermute(emp, "space", swap)]
            traded = lax.ppermute(emp, "tm", [(0, 1), (1, 0)]) if splits > 1 else None
        elif hop == 3:
            from_left, from_right, traded = lax.optimization_barrier((from_left, from_right, traded))
            if splits > 1:
                emp_parts += [traded, lax.ppermute(traded, "space", swap)]
            held_times = hold(times, (from_left, from_right))
            every_time = [times] + [
                lax.ppermute(held_times, "tm", [((d + step) % tm, d) for d in range(tm)]) for step in range(1, tm)
            ]
        elif hop == 4:
            from_left, from_right, every_time = lax.optimization_barrier((from_left, from_right, every_time))
            scalars = jnp.concatenate([gaps] + every_time + [cos_weights.reshape(-1)])
            weights = all_pair_weights(
                place, hold(scalars, (from_left, from_right)), tm, own_count, time_count, own_occ, own_emp
            )
        elif hop > 4:
            from_left, from_right = lax.optimization_barrier((from_left, from_right))
        from_left = lax.ppermute(from_left, "space", ahead)
        found.append(from_left)
        offsets.append(-hop)
        if 2 * hop < chips:
            from_right = lax.ppermute(from_right, "space", back)
            found.append(from_right)
            offsets.append(hop)

    results = []
    part_rows = NG // space
    for w in range(own_count):
        keep_far, send_far, keep_near, send_near = pair_moment(
            place, weights[w], found, offsets, emp_parts, tables
        )
        far_total = keep_far + lax.ppermute(send_far, "space", swap).astype(jnp.float32)
        near_total = keep_near + lax.ppermute(send_near, "space", swap).astype(jnp.float32)
        far = far_slots(chips)
        near = [slot for slot in range(chips) if slot not in far]
        totals = {}
        for slots, total in ((far, far_total), (near, near_total)):
            for index, slot in enumerate(slots):
                start = index * round_up(part_rows, 16)
                totals[slot] = total[start : start + part_rows]
        results.append(reduce_ring(totals, chips))
    return jnp.stack(results)


def solution(mesh):
    return jax.shard_map(
        functools.partial(local, mesh.shape["space"], mesh.shape["tm"]),
        mesh=mesh,
        in_specs=(P("space", None), P(), P("tm"), P()),
        out_specs=P("tm", "space", None),
        check_vma=False,
    )
```

```python
import functools
import math

import jax
import jax.numpy as jnp
from jax import lax
from jax.experimental import pallas as pl
from jax.experimental.pallas import tpu as pltpu
from jax.sharding import PartitionSpec as P

SIDE = 24
NG = 864
NOCC = 64
NEMP = 256
LANES = 128
PLANES = 3


def round_up(value, step):
    return -(-value // step) * step


def pair_weights(tm, own_count, time_count, n_occ, n_emp, place_ref, scalar_ref, out_ref):
    me, tm_index = place_ref[0], place_ref[1]
    core, own_chip = lax.rem(me, 2), lax.div(me, 2)
    shape = out_ref.shape[1:]
    pair = lax.broadcasted_iota(jnp.int32, shape, 0) * LANES + lax.broadcasted_iota(jnp.int32, shape, 1)
    occ_number = lax.rem(pair, n_occ)
    occ_gap = jnp.zeros(shape, jnp.float32)
    emp_gap = jnp.zeros(shape, jnp.float32)
    for i in range(n_occ):
        occ_gap = jnp.where(occ_number == i, scalar_ref[core * n_occ + i], occ_gap)
    for j in range(n_emp):
        emp_gap = jnp.where(pair >= j * n_occ, scalar_ref[NOCC + own_chip * n_emp + j], emp_gap)
    first_time = NOCC + NEMP
    first_share = first_time + time_count
    weights = [jnp.zeros(shape, jnp.float32) for _ in range(own_count)]
    for k in range(time_count):
        hop, number = divmod(k, time_count // tm)
        source = lax.rem(tm_index + hop, tm) * (time_count // tm) + number
        time = scalar_ref[first_time + k]
        occ_factor = jnp.exp(-occ_gap * time) * NOCC ** (-0.5)
        emp_factor = jnp.exp(-emp_gap * time) * NEMP ** (-0.5)
        for w in range(own_count):
            share = scalar_ref[first_share + (tm_index * own_count + w) * time_count + source]
            weights[w] = weights[w] + share * (occ_factor * emp_factor)
    for w in range(own_count):
        out_ref[w] = weights[w]


def table_kernel(held_ref, out_ref, with_cos, with_sin):
    kind = pl.program_id(0) + held_ref[0]
    a_odd, b_odd = kind // 2, kind % 2
    half = SIDE // 2
    a_waves, b_waves, c_waves = SIDE // 4, SIDE // 8, NG // (SIDE // 2 * (SIDE // 4) * 2)
    width = out_ref.shape[2]

    def parts(value, size):
        whole = jnp.floor((value + 0.5) * (1.0 / size))
        return whole, value - size * whole

    column = lax.broadcasted_iota(jnp.int32, (SIDE, width), 1).astype(jnp.float32)
    row = lax.broadcasted_iota(jnp.int32, (SIDE, width), 0).astype(jnp.float32)
    a_step, rest = parts(column, 2 * c_waves * b_waves)
    sine, rest = parts(rest, c_waves * b_waves)
    c_step, b_step = parts(rest, b_waves)
    a = 2.0 * a_step + ((a_odd + a_waves) % 2 - a_waves).astype(jnp.float32)
    b = 2.0 * b_step + ((b_odd + b_waves) % 2 - b_waves).astype(jnp.float32)
    c = c_step + 1.0
    unit = 2.0 * math.pi / SIDE
    size = jnp.where(a_step < a_waves, math.sqrt(2.0 / SIDE**3), 0.0)

    def factors(wave):
        angle = parts(wave * row, SIDE)[1] * unit
        return jnp.cos(angle), jnp.sin(angle)

    cos_p, sin_p = factors(a)
    cos_q, sin_q = factors(b)
    cos_s, sin_s = factors(c)
    is_sine = sine > 0.5
    for y in range(half):
        inner_cos = cos_q[y : y + 1] * cos_s - sin_q[y : y + 1] * sin_s
        inner_sin = sin_q[y : y + 1] * cos_s + cos_q[y : y + 1] * sin_s
        rows = slice(y * SIDE, (y + 1) * SIDE)
        with_cos[rows] = jnp.where(is_sine, inner_sin, inner_cos) * size
        with_sin[rows] = jnp.where(is_sine, inner_cos, -inner_sin) * size
    plane = half * SIDE
    depth = round_up(PLANES * plane, LANES)
    for x in range(half):
        start = x // PLANES * depth + x % PLANES * plane
        table = cos_p[x : x + 1] * with_cos[...] + sin_p[x : x + 1] * with_sin[...]
        out_ref[0, start : start + plane] = table.astype(jnp.bfloat16)
    for step in range(half // PLANES):
        out_ref[0, step * depth + PLANES * plane : (step + 1) * depth] = jnp.zeros(
            (depth - PLANES * plane, width), jnp.bfloat16
        )


def class_tables(held):
    plane = SIDE * SIDE // 2
    depth = SIDE // 2 // PLANES * round_up(PLANES * plane, LANES)
    width = round_up(NG // 4, 2 * LANES)
    return pl.pallas_call(
        table_kernel,
        grid=(4,),
        out_shape=jax.ShapeDtypeStruct((4, depth, width), jnp.bfloat16),
        in_specs=[pl.BlockSpec(memory_space=pltpu.SMEM)],
        out_specs=pl.BlockSpec((1, depth, width), lambda k: (k, 0, 0)),
        scratch_shapes=[pltpu.VMEM((plane, width), jnp.float32), pltpu.VMEM((plane, width), jnp.float32)],
        compiler_params=pltpu.CompilerParams(vmem_limit_bytes=60 * 1024 * 1024),
        cost_estimate=pl.CostEstimate(
            flops=64 * depth * width, bytes_accessed=8 * depth * width, transcendentals=0
        ),
        name="class_tables",
    )(held)


def all_pair_weights(place, scalars, tm, own_count, time_count, n_occ, n_emp):
    smem = pl.BlockSpec(memory_space=pltpu.SMEM)
    return pl.pallas_call(
        functools.partial(pair_weights, tm, own_count, time_count, n_occ, n_emp),
        out_shape=jax.ShapeDtypeStruct((own_count, n_occ * n_emp // LANES, LANES), jnp.float32),
        in_specs=[smem, smem],
        out_specs=pl.BlockSpec(memory_space=pltpu.VMEM),
        cost_estimate=pl.CostEstimate(flops=2**24, bytes_accessed=2**20, transcendentals=0),
        name="pair_weights",
    )(place, scalars)


def ring_place(chip, chips):
    return jnp.where(chip % 2 == 0, chip // 2, chips - (chip + 1) // 2)


def ring_chip(place, chips):
    place = lax.rem(place + chips, chips)
    return jnp.where(place < chips // 2, 2 * place, 2 * (chips - place) - 1)


def far_slots(chips):
    return [chips // 2, chips // 2 + 1]


def pair_kernel(offsets, splits, place_ref, weight_ref, *refs):
    emp_refs, refs = refs[: 2 * splits], refs[2 * splits :]
    chips, part_emp, n_rows = emp_refs[0].shape
    n_emp = splits * part_emp
    shards = 2 * chips
    occ_refs, refs = refs[:chips], refs[chips:]
    table_hbm, keep_far, send_far, keep_near, send_near = refs[:5]
    occ_wide, emp_wide, rho, table, table_sem, raw_sem = refs[5:]
    depth = round_up(PLANES * SIDE * SIDE // 2, LANES)
    steps = table.shape[1] // depth
    n_occ = occ_wide.shape[1]
    per_group = chips // steps
    plane = SIDE * SIDE // 2

    copy = pltpu.make_async_copy(table_hbm, table, table_sem)
    me = place_ref[0]
    core, own_chip = lax.rem(me, 2), lax.div(me, 2)
    place = ring_place(own_chip, chips)

    def low_and_high(raw, rows, target):
        for far in range(2):
            for step in range(steps):
                group = far * steps + step
                first_chip = group * per_group // 2
                shard_rows = [
                    raw[first_chip + shard // 2, shard % 2, rows] for shard in range(per_group)
                ]
                for upper in range(2):
                    pieces = []
                    for x in range(PLANES):
                        start = (2 * x + upper) * plane
                        stop = start + plane
                        while start < stop:
                            shard, offset = divmod(start, n_rows)
                            count = min(stop - start, n_rows - offset)
                            pieces.append(shard_rows[shard][:, offset : offset + count])
                            start += count
                    pieces.append(jnp.zeros((pieces[0].shape[0], depth - PLANES * plane), raw.dtype))
                    lanes = slice(step * depth, (step + 1) * depth)
                    target[2 * far + upper, rows, lanes] = jnp.concatenate(pieces, axis=1).astype(target.dtype)

    def arrange(raw_occ, raw_emp):
        copies = []
        for index, (offset, ref) in enumerate(zip(offsets, occ_refs, strict=True)):
            chip = ring_chip(place + offset, chips)
            for other in range(2):
                target = raw_occ.at[chip, 1 - core if other else core]
                copies.append(pltpu.make_async_copy(ref.at[other], target, raw_sem.at[2 * index + other]))
        for index, ref in enumerate(emp_refs):
            part, other = divmod(index, 2)
            start = pl.multiple_of(lax.rem(place_ref[1] + part, splits) * part_emp, part_emp)
            target = raw_emp.at[:, 1 - core if other else core, pl.ds(start, part_emp)]
            copies.append(pltpu.make_async_copy(ref, target, raw_sem.at[shards + index]))
        for raw_copy in copies:
            raw_copy.start()
        for raw_copy in copies:
            raw_copy.wait()
        copy.start()

        def sixteen(raw, target):
            def rows(part, carry):
                low_and_high(raw, pl.ds(pl.multiple_of(part * 16, 16), 16), target)
                return carry

            lax.fori_loop(0, raw.shape[2] // 16, rows, 0)

        sixteen(raw_occ, occ_wide)
        sixteen(raw_emp, emp_wide)

    pl.run_scoped(
        arrange,
        pltpu.VMEM((chips, 2, n_occ, n_rows), jnp.bfloat16),
        pltpu.VMEM((chips, 2, n_emp, n_rows), jnp.bfloat16),
    )

    def build(target, cut):
        emp_rows = [emp_wide[k, :, cut] for k in range(4)]
        for i in range(n_emp):
            emp_row = [
                jnp.broadcast_to(emp_rows[k][i : i + 1], (16, LANES)).astype(jnp.bfloat16) for k in range(4)
            ]
            for part in range(0, n_occ, 16):
                near_low, near_high, far_low, far_high = (
                    emp_row[k] * occ_wide[k, part : part + 16, cut] for k in range(4)
                )
                even_low, odd_low = near_low + far_low, near_low - far_low
                even_high, odd_high = near_high + far_high, near_high - far_high
                rows = slice(i * n_occ + part, i * n_occ + part + 16)
                target[0, rows, cut] = even_low + even_high
                target[1, rows, cut] = even_low - even_high
                target[2, rows, cut] = odd_low + odd_high
                target[3, rows, cut] = odd_low - odd_high

    modes = rho.shape[1]
    spacing = SIDE
    per_a = modes // spacing

    def multiply(source, k):
        found = jnp.dot(source[k], table[k], preferred_element_type=jnp.float32).T
        a_odd, b_odd = divmod(k, 2)
        a_first = (a_odd + SIDE // 4) % 2
        b_first = (b_odd + SIDE // 8) % 2
        for a_step in range(SIDE // 4):
            start = b_first * (SIDE // 2) + 2 * a_step + a_first
            for tile in range(source.shape[1] // LANES):
                rho[tile, pl.ds(start, per_a, stride=spacing), :] = found[
                    a_step * per_a : (a_step + 1) * per_a, tile * LANES : (tile + 1) * LANES
                ]

    chunks = steps * depth // LANES

    def transform(products):
        def build_chunk(chunk, carry):
            build(products, pl.ds(pl.multiple_of(chunk * LANES, LANES), LANES))
            return carry

        lax.fori_loop(0, chunks, build_chunk, 0)
        copy.wait()
        for k in range(4):
            multiply(products, k)

    pl.run_scoped(transform, pltpu.VMEM((4, n_emp * n_occ, steps * depth), jnp.bfloat16))

    rows = NG // shards

    def combine(blocks):
        tiles = range(rho.shape[0])
        ordered = jnp.concatenate([rho[tile].astype(jnp.bfloat16) for tile in tiles], axis=1)
        weighted = jnp.concatenate(
            [(rho[tile] * weight_ref[tile : tile + 1]).astype(jnp.bfloat16) for tile in tiles], axis=1
        )
        moment = lax.dot_general(
            weighted, ordered, (((1,), (1,)), ((), ())), preferred_element_type=jnp.float32
        )
        for k in range(shards):
            blocks[k] = moment[k * rows : (k + 1) * rows]
        far = far_slots(chips)
        near = [slot for slot in range(chips) if slot not in far]
        for slots, keep, send in ((far, keep_far, send_far), (near, keep_near, send_near)):
            for index, slot in enumerate(slots):
                chip = ring_chip(place + slot, chips)
                start = index * round_up(rows, 16)
                keep[start : start + rows, :NG] = blocks[2 * chip + core]
                send[start : start + rows, :NG] = blocks[2 * chip + 1 - core].astype(jnp.bfloat16)

    pl.run_scoped(combine, pltpu.VMEM((shards, rows, NG), jnp.float32))


def pair_moment(place, weights, occ_blocks, offsets, emp_parts, tables):
    splits = len(emp_parts) // 2
    chips, part_emp, _ = emp_parts[0].shape
    n_emp = splits * part_emp
    n_occ = occ_blocks[0].shape[1]
    _, depth, width = tables.shape
    pairs = n_occ * n_emp
    rows = NG // (2 * chips)
    far_rows, near_rows = 2 * round_up(rows, 16), (chips - 2) * round_up(rows, 16)
    smem = pl.BlockSpec(memory_space=pltpu.SMEM)
    vmem = pl.BlockSpec(memory_space=pltpu.VMEM)
    hbm = pl.BlockSpec(memory_space=pl.ANY)
    return pl.pallas_call(
        functools.partial(pair_kernel, offsets, splits),
        out_shape=tuple(
            jax.ShapeDtypeStruct((count, round_up(NG, LANES)), dtype)
            for count in (far_rows, near_rows)
            for dtype in (jnp.float32, jnp.bfloat16)
        ),
        in_specs=[smem, vmem] + [hbm] * (2 * splits + chips + 1),
        out_specs=(vmem, vmem, vmem, vmem),
        scratch_shapes=[
            pltpu.VMEM((4, n_occ, depth), jnp.bfloat16),
            pltpu.VMEM((4, n_emp, depth), jnp.float32),
            pltpu.VMEM((pairs // LANES, NG, LANES), jnp.float32),
            pltpu.VMEM((4, depth, width), jnp.bfloat16),
            pltpu.SemaphoreType.DMA,
            pltpu.SemaphoreType.DMA((2 * chips + 2 * splits,)),
        ],
        compiler_params=pltpu.CompilerParams(vmem_limit_bytes=60 * 1024 * 1024),
        cost_estimate=pl.CostEstimate(
            flops=8 * pairs * depth * width, bytes_accessed=16 * 2**20, transcendentals=0
        ),
        name="pair_moment",
    )(place, weights, *emp_parts, *occ_blocks, tables)


def ring_steps(chips):
    ring = list(range(0, chips, 2)) + list(range(chips - 1, 0, -2))
    ahead = [
        (2 * ring[k] + core, 2 * ring[(k + 1) % chips] + core) for k in range(chips) for core in range(2)
    ]
    return ahead, [(to, start) for start, to in ahead]


def hold(value, until):
    return lax.optimization_barrier((value, until))[0]


def reduce_ring(totals, chips):
    ahead, back = ring_steps(chips)
    farthest = chips // 2
    from_left, from_right = totals[farthest], totals[farthest + 1]
    for hop in range(1, farthest + 1):
        from_left = lax.ppermute(from_left.astype(jnp.bfloat16), "space", ahead).astype(jnp.float32)
        if hop < farthest:
            from_right = lax.ppermute(from_right.astype(jnp.bfloat16), "space", back).astype(jnp.float32)
            from_left = from_left + totals[farthest - hop]
        if hop < farthest - 1:
            from_right = from_right + totals[farthest + 1 + hop]
    return (totals[0] + from_left + from_right)[:, :NG]


def local(space, tm, orbitals, gaps, times, cos_weights):
    rows = orbitals.shape[0]
    chips = space // 2
    columns = orbitals.T
    own_occ, own_emp = NOCC // 2, NEMP // chips
    own_count, time_count = cos_weights.shape[0] // tm, cos_weights.shape[1]
    me = lax.axis_index("space")
    core = me % 2
    swap = [(d, d ^ 1) for d in range(space)]

    place = jnp.stack([me, lax.axis_index("tm")]).astype(jnp.int32)

    occ = columns[:NOCC].reshape(2, own_occ, rows)
    occ_mine = lax.dynamic_index_in_dim(occ, core, 0, keepdims=False)
    occ_theirs = lax.dynamic_index_in_dim(occ, 1 - core, 0, keepdims=False)
    occ_pair = jnp.stack([occ_mine, lax.ppermute(occ_theirs, "space", swap)])
    splits = tm if tm == 2 else 1
    emp_columns = lax.dynamic_slice(
        columns.reshape((NOCC + NEMP) // own_emp, splits, own_emp // splits, rows),
        (NOCC // own_emp, lax.axis_index("tm") % splits, 0, 0),
        (chips, 1, own_emp // splits, rows),
    )
    emp = lax.all_to_all(
        emp_columns.reshape(chips, own_emp // splits, rows),
        "space",
        split_axis=0,
        concat_axis=0,
        axis_index_groups=[[2 * k + c for k in range(chips)] for c in range(2)],
    )

    tables = class_tables(hold(jnp.zeros((1,), jnp.int32), occ_pair))
    emp_parts = []
    ahead, back = ring_steps(chips)
    found, offsets = [occ_pair], [0]
    from_left = from_right = occ_pair
    for hop in range(1, chips // 2 + 1):
        if hop == 2:
            from_left, from_right, emp, tables = lax.optimization_barrier((from_left, from_right, emp, tables))
            traded = lax.ppermute(emp, "tm", [(0, 1), (1, 0)]) if splits > 1 else None
        elif hop == 3:
            from_left, from_right, emp, traded = lax.optimization_barrier((from_left, from_right, emp, traded))
            emp_parts += [emp, lax.ppermute(emp, "space", swap)]
            if splits > 1:
                emp_parts += [traded, lax.ppermute(traded, "space", swap)]
            held_times = hold(times, (from_left, from_right))
            every_time = [times] + [
                lax.ppermute(held_times, "tm", [((d + step) % tm, d) for d in range(tm)]) for step in range(1, tm)
            ]
        elif hop == 4:
            from_left, from_right = lax.optimization_barrier((from_left, from_right))
            scalars = jnp.concatenate([gaps] + every_time + [cos_weights.reshape(-1)])
            weights = all_pair_weights(
                place, hold(scalars, (from_left, from_right)), tm, own_count, time_count, own_occ, own_emp
            )
        elif hop > 4:
            from_left, from_right = lax.optimization_barrier((from_left, from_right))
        from_left = lax.ppermute(from_left, "space", ahead)
        found.append(from_left)
        offsets.append(-hop)
        if 2 * hop < chips:
            from_right = lax.ppermute(from_right, "space", back)
            found.append(from_right)
            offsets.append(hop)

    results = []
    part_rows = NG // space
    for w in range(own_count):
        keep_far, send_far, keep_near, send_near = pair_moment(
            place, weights[w], found, offsets, emp_parts, tables
        )
        far_total = keep_far + lax.ppermute(send_far, "space", swap).astype(jnp.float32)
        near_total = keep_near + lax.ppermute(send_near, "space", swap).astype(jnp.float32)
        far = far_slots(chips)
        near = [slot for slot in range(chips) if slot not in far]
        totals = {}
        for slots, total in ((far, far_total), (near, near_total)):
            for index, slot in enumerate(slots):
                start = index * round_up(part_rows, 16)
                totals[slot] = total[start : start + part_rows]
        results.append(reduce_ring(totals, chips))
    return jnp.stack(results)


def solution(mesh):
    return jax.shard_map(
        functools.partial(local, mesh.shape["space"], mesh.shape["tm"]),
        mesh=mesh,
        in_specs=(P("space", None), P(), P("tm"), P()),
        out_specs=P("tm", "space", None),
        check_vma=False,
    )
```

```python
import functools
import math

import jax
import jax.numpy as jnp
from jax import lax
from jax.experimental import pallas as pl
from jax.experimental.pallas import tpu as pltpu
from jax.sharding import PartitionSpec as P

SIDE = 24
NG = 864
NOCC = 64
NEMP = 256
LANES = 128
PLANES = 3


def round_up(value, step):
    return -(-value // step) * step


def pair_weights(tm, own_count, time_count, n_occ, n_emp, place_ref, scalar_ref, out_ref):
    me, tm_index = place_ref[0], place_ref[1]
    core, own_chip = lax.rem(me, 2), lax.div(me, 2)
    shape = out_ref.shape[1:]
    pair = lax.broadcasted_iota(jnp.int32, shape, 0) * LANES + lax.broadcasted_iota(jnp.int32, shape, 1)
    occ_number = lax.rem(pair, n_occ)
    occ_gap = jnp.zeros(shape, jnp.float32)
    emp_gap = jnp.zeros(shape, jnp.float32)
    for i in range(n_occ):
        occ_gap = jnp.where(occ_number == i, scalar_ref[core * n_occ + i], occ_gap)
    for j in range(n_emp):
        emp_gap = jnp.where(pair >= j * n_occ, scalar_ref[NOCC + own_chip * n_emp + j], emp_gap)
    first_time = NOCC + NEMP
    first_share = first_time + time_count
    weights = [jnp.zeros(shape, jnp.float32) for _ in range(own_count)]
    for k in range(time_count):
        hop, number = divmod(k, time_count // tm)
        source = lax.rem(tm_index + hop, tm) * (time_count // tm) + number
        time = scalar_ref[first_time + k]
        occ_factor = jnp.exp(-occ_gap * time) * NOCC ** (-0.5)
        emp_factor = jnp.exp(-emp_gap * time) * NEMP ** (-0.5)
        for w in range(own_count):
            share = scalar_ref[first_share + (tm_index * own_count + w) * time_count + source]
            weights[w] = weights[w] + share * (occ_factor * emp_factor)
    for w in range(own_count):
        out_ref[w] = weights[w]


def table_kernel(held_ref, out_ref, with_cos, with_sin):
    kind = pl.program_id(0) + held_ref[0]
    a_odd, b_odd = kind // 2, kind % 2
    half = SIDE // 2
    a_waves, b_waves, c_waves = SIDE // 4, SIDE // 8, NG // (SIDE // 2 * (SIDE // 4) * 2)
    width = out_ref.shape[2]

    def parts(value, size):
        whole = jnp.floor((value + 0.5) * (1.0 / size))
        return whole, value - size * whole

    column = lax.broadcasted_iota(jnp.int32, (SIDE, width), 1).astype(jnp.float32)
    row = lax.broadcasted_iota(jnp.int32, (SIDE, width), 0).astype(jnp.float32)
    a_step, rest = parts(column, 2 * c_waves * b_waves)
    sine, rest = parts(rest, c_waves * b_waves)
    c_step, b_step = parts(rest, b_waves)
    a = 2.0 * a_step + ((a_odd + a_waves) % 2 - a_waves).astype(jnp.float32)
    b = 2.0 * b_step + ((b_odd + b_waves) % 2 - b_waves).astype(jnp.float32)
    c = c_step + 1.0
    unit = 2.0 * math.pi / SIDE
    size = jnp.where(a_step < a_waves, math.sqrt(2.0 / SIDE**3), 0.0)

    def factors(wave):
        angle = parts(wave * row, SIDE)[1] * unit
        return jnp.cos(angle), jnp.sin(angle)

    cos_p, sin_p = factors(a)
    cos_q, sin_q = factors(b)
    cos_s, sin_s = factors(c)
    is_sine = sine > 0.5
    for y in range(half):
        inner_cos = cos_q[y : y + 1] * cos_s - sin_q[y : y + 1] * sin_s
        inner_sin = sin_q[y : y + 1] * cos_s + cos_q[y : y + 1] * sin_s
        rows = slice(y * SIDE, (y + 1) * SIDE)
        with_cos[rows] = jnp.where(is_sine, inner_sin, inner_cos) * size
        with_sin[rows] = jnp.where(is_sine, inner_cos, -inner_sin) * size
    plane = half * SIDE
    depth = round_up(PLANES * plane, LANES)
    for x in range(half):
        start = x // PLANES * depth + x % PLANES * plane
        table = cos_p[x : x + 1] * with_cos[...] + sin_p[x : x + 1] * with_sin[...]
        out_ref[0, start : start + plane] = table.astype(jnp.bfloat16)
    for step in range(half // PLANES):
        out_ref[0, step * depth + PLANES * plane : (step + 1) * depth] = jnp.zeros(
            (depth - PLANES * plane, width), jnp.bfloat16
        )


def class_tables(held):
    plane = SIDE * SIDE // 2
    depth = SIDE // 2 // PLANES * round_up(PLANES * plane, LANES)
    width = round_up(NG // 4, 2 * LANES)
    return pl.pallas_call(
        table_kernel,
        grid=(4,),
        out_shape=jax.ShapeDtypeStruct((4, depth, width), jnp.bfloat16),
        in_specs=[pl.BlockSpec(memory_space=pltpu.SMEM)],
        out_specs=pl.BlockSpec((1, depth, width), lambda k: (k, 0, 0)),
        scratch_shapes=[pltpu.VMEM((plane, width), jnp.float32), pltpu.VMEM((plane, width), jnp.float32)],
        compiler_params=pltpu.CompilerParams(vmem_limit_bytes=60 * 1024 * 1024),
        cost_estimate=pl.CostEstimate(
            flops=64 * depth * width, bytes_accessed=8 * depth * width, transcendentals=0
        ),
        name="class_tables",
    )(held)


def all_pair_weights(place, scalars, tm, own_count, time_count, n_occ, n_emp):
    smem = pl.BlockSpec(memory_space=pltpu.SMEM)
    return pl.pallas_call(
        functools.partial(pair_weights, tm, own_count, time_count, n_occ, n_emp),
        out_shape=jax.ShapeDtypeStruct((own_count, n_occ * n_emp // LANES, LANES), jnp.float32),
        in_specs=[smem, smem],
        out_specs=pl.BlockSpec(memory_space=pltpu.VMEM),
        cost_estimate=pl.CostEstimate(flops=2**24, bytes_accessed=2**20, transcendentals=0),
        name="pair_weights",
    )(place, scalars)


def ring_place(chip, chips):
    return jnp.where(chip % 2 == 0, chip // 2, chips - (chip + 1) // 2)


def ring_chip(place, chips):
    place = lax.rem(place + chips, chips)
    return jnp.where(place < chips // 2, 2 * place, 2 * (chips - place) - 1)


def far_slots(chips):
    return [chips // 2, chips // 2 + 1]


def pair_kernel(offsets, splits, place_ref, weight_ref, *refs):
    emp_refs, refs = refs[: 2 * splits], refs[2 * splits :]
    chips, part_emp, n_rows = emp_refs[0].shape
    n_emp = splits * part_emp
    shards = 2 * chips
    occ_refs, refs = refs[:chips], refs[chips:]
    table_hbm, keep_far, send_far, keep_near, send_near = refs[:5]
    occ_wide, emp_wide, rho, table, table_sem, raw_sem = refs[5:]
    depth = round_up(PLANES * SIDE * SIDE // 2, LANES)
    steps = table.shape[1] // depth
    n_occ = occ_wide.shape[1]
    per_group = chips // steps
    plane = SIDE * SIDE // 2
    whole_rows = max(1, LANES // n_occ)
    first_emp = max(1, 3 * n_emp // 8 // whole_rows) * whole_rows
    emp_cuts = (slice(0, first_emp), slice(first_emp, n_emp))

    copy = pltpu.make_async_copy(table_hbm, table, table_sem)
    me = place_ref[0]
    core, own_chip = lax.rem(me, 2), lax.div(me, 2)
    place = ring_place(own_chip, chips)

    def low_and_high(raw, rows, target):
        for far in range(2):
            for step in range(steps):
                group = far * steps + step
                first_chip = group * per_group // 2
                shard_rows = [
                    raw[first_chip + shard // 2, shard % 2, rows] for shard in range(per_group)
                ]
                for upper in range(2):
                    pieces = []
                    for x in range(PLANES):
                        start = (2 * x + upper) * plane
                        stop = start + plane
                        while start < stop:
                            shard, offset = divmod(start, n_rows)
                            count = min(stop - start, n_rows - offset)
                            pieces.append(shard_rows[shard][:, offset : offset + count])
                            start += count
                    pieces.append(jnp.zeros((pieces[0].shape[0], depth - PLANES * plane), raw.dtype))
                    lanes = slice(step * depth, (step + 1) * depth)
                    target[2 * far + upper, rows, lanes] = jnp.concatenate(pieces, axis=1).astype(target.dtype)

    def arrange(raw_occ, raw_emp):
        copies = []
        for index, (offset, ref) in enumerate(zip(offsets, occ_refs, strict=True)):
            chip = ring_chip(place + offset, chips)
            for other in range(2):
                target = raw_occ.at[chip, 1 - core if other else core]
                copies.append(pltpu.make_async_copy(ref.at[other], target, raw_sem.at[2 * index + other]))
        for index, ref in enumerate(emp_refs):
            part, other = divmod(index, 2)
            start = pl.multiple_of(lax.rem(place_ref[1] + part, splits) * part_emp, part_emp)
            target = raw_emp.at[:, 1 - core if other else core, pl.ds(start, part_emp)]
            copies.append(pltpu.make_async_copy(ref, target, raw_sem.at[shards + index]))
        for raw_copy in copies:
            raw_copy.start()
        for raw_copy in copies:
            raw_copy.wait()
        copy.start()

        def sixteen(raw, target):
            def rows(part, carry):
                low_and_high(raw, pl.ds(pl.multiple_of(part * 16, 16), 16), target)
                return carry

            lax.fori_loop(0, raw.shape[2] // 16, rows, 0)

        sixteen(raw_occ, occ_wide)
        sixteen(raw_emp, emp_wide)

    pl.run_scoped(
        arrange,
        pltpu.VMEM((chips, 2, n_occ, n_rows), jnp.bfloat16),
        pltpu.VMEM((chips, 2, n_emp, n_rows), jnp.bfloat16),
    )

    def build(half, target, cut):
        emp_rows = [emp_wide[k, emp_cuts[half], cut] for k in range(4)]
        for i in range(emp_rows[0].shape[0]):
            emp_row = [
                jnp.broadcast_to(emp_rows[k][i : i + 1], (16, LANES)).astype(jnp.bfloat16) for k in range(4)
            ]
            for part in range(0, n_occ, 16):
                near_low, near_high, far_low, far_high = (
                    emp_row[k] * occ_wide[k, part : part + 16, cut] for k in range(4)
                )
                even_low, odd_low = near_low + far_low, near_low - far_low
                even_high, odd_high = near_high + far_high, near_high - far_high
                rows = slice(i * n_occ + part, i * n_occ + part + 16)
                target[0, rows, cut] = even_low + even_high
                target[1, rows, cut] = even_low - even_high
                target[2, rows, cut] = odd_low + odd_high
                target[3, rows, cut] = odd_low - odd_high

    modes = rho.shape[1]
    spacing = SIDE
    per_a = modes // spacing

    def multiply(half, source, k):
        found = jnp.dot(source[k], table[k], preferred_element_type=jnp.float32).T
        a_odd, b_odd = divmod(k, 2)
        a_first = (a_odd + SIDE // 4) % 2
        b_first = (b_odd + SIDE // 8) % 2
        for a_step in range(SIDE // 4):
            start = b_first * (SIDE // 2) + 2 * a_step + a_first
            for tile in range(source.shape[1] // LANES):
                rho[emp_cuts[half].start * n_occ // LANES + tile, pl.ds(start, per_a, stride=spacing), :] = found[
                    a_step * per_a : (a_step + 1) * per_a, tile * LANES : (tile + 1) * LANES
                ]

    chunks = steps * depth // LANES

    def transform(first, second):
        def build_first(chunk, carry):
            build(0, first, pl.ds(pl.multiple_of(chunk * LANES, LANES), LANES))
            return carry

        lax.fori_loop(0, chunks, build_first, 0)
        copy.wait()
        for k in range(4):
            for chunk in range(k * chunks // 4, (k + 1) * chunks // 4):
                build(1, second, slice(chunk * LANES, (chunk + 1) * LANES))
            multiply(0, first, k)
        for k in range(4):
            multiply(1, second, k)

    pl.run_scoped(
        transform,
        *(
            pltpu.VMEM((4, (cut.stop - cut.start) * n_occ, steps * depth), jnp.bfloat16) for cut in emp_cuts
        ),
    )

    rows = NG // shards

    def combine(blocks):
        tiles = range(rho.shape[0])
        ordered = jnp.concatenate([rho[tile].astype(jnp.bfloat16) for tile in tiles], axis=1)
        weighted = jnp.concatenate(
            [(rho[tile] * weight_ref[tile : tile + 1]).astype(jnp.bfloat16) for tile in tiles], axis=1
        )
        moment = lax.dot_general(
            weighted, ordered, (((1,), (1,)), ((), ())), preferred_element_type=jnp.float32
        )
        for k in range(shards):
            blocks[k] = moment[k * rows : (k + 1) * rows]
        far = far_slots(chips)
        near = [slot for slot in range(chips) if slot not in far]
        for slots, keep, send in ((far, keep_far, send_far), (near, keep_near, send_near)):
            for index, slot in enumerate(slots):
                chip = ring_chip(place + slot, chips)
                start = index * round_up(rows, 16)
                keep[start : start + rows, :NG] = blocks[2 * chip + core]
                send[start : start + rows, :NG] = blocks[2 * chip + 1 - core].astype(jnp.bfloat16)

    pl.run_scoped(combine, pltpu.VMEM((shards, rows, NG), jnp.float32))


def pair_moment(place, weights, occ_blocks, offsets, emp_parts, tables):
    splits = len(emp_parts) // 2
    chips, part_emp, _ = emp_parts[0].shape
    n_emp = splits * part_emp
    n_occ = occ_blocks[0].shape[1]
    _, depth, width = tables.shape
    pairs = n_occ * n_emp
    rows = NG // (2 * chips)
    far_rows, near_rows = 2 * round_up(rows, 16), (chips - 2) * round_up(rows, 16)
    smem = pl.BlockSpec(memory_space=pltpu.SMEM)
    vmem = pl.BlockSpec(memory_space=pltpu.VMEM)
    hbm = pl.BlockSpec(memory_space=pl.ANY)
    return pl.pallas_call(
        functools.partial(pair_kernel, offsets, splits),
        out_shape=tuple(
            jax.ShapeDtypeStruct((count, round_up(NG, LANES)), dtype)
            for count in (far_rows, near_rows)
            for dtype in (jnp.float32, jnp.bfloat16)
        ),
        in_specs=[smem, vmem] + [hbm] * (2 * splits + chips + 1),
        out_specs=(vmem, vmem, vmem, vmem),
        scratch_shapes=[
            pltpu.VMEM((4, n_occ, depth), jnp.bfloat16),
            pltpu.VMEM((4, n_emp, depth), jnp.float32),
            pltpu.VMEM((pairs // LANES, NG, LANES), jnp.float32),
            pltpu.VMEM((4, depth, width), jnp.bfloat16),
            pltpu.SemaphoreType.DMA,
            pltpu.SemaphoreType.DMA((2 * chips + 2 * splits,)),
        ],
        compiler_params=pltpu.CompilerParams(vmem_limit_bytes=60 * 1024 * 1024),
        cost_estimate=pl.CostEstimate(
            flops=8 * pairs * depth * width, bytes_accessed=16 * 2**20, transcendentals=0
        ),
        name="pair_moment",
    )(place, weights, *emp_parts, *occ_blocks, tables)


def ring_steps(chips):
    ring = list(range(0, chips, 2)) + list(range(chips - 1, 0, -2))
    ahead = [
        (2 * ring[k] + core, 2 * ring[(k + 1) % chips] + core) for k in range(chips) for core in range(2)
    ]
    return ahead, [(to, start) for start, to in ahead]


def hold(value, until):
    return lax.optimization_barrier((value, until))[0]


def reduce_ring(totals, chips):
    ahead, back = ring_steps(chips)
    farthest = chips // 2
    from_left, from_right = totals[farthest], totals[farthest + 1]
    for hop in range(1, farthest + 1):
        from_left = lax.ppermute(from_left.astype(jnp.bfloat16), "space", ahead).astype(jnp.float32)
        if hop < farthest:
            from_right = lax.ppermute(from_right.astype(jnp.bfloat16), "space", back).astype(jnp.float32)
            from_left = from_left + totals[farthest - hop]
        if hop < farthest - 1:
            from_right = from_right + totals[farthest + 1 + hop]
    return (totals[0] + from_left + from_right)[:, :NG]


def local(space, tm, orbitals, gaps, times, cos_weights):
    rows = orbitals.shape[0]
    chips = space // 2
    columns = orbitals.T
    own_occ, own_emp = NOCC // 2, NEMP // chips
    own_count, time_count = cos_weights.shape[0] // tm, cos_weights.shape[1]
    me = lax.axis_index("space")
    core = me % 2
    swap = [(d, d ^ 1) for d in range(space)]

    place = jnp.stack([me, lax.axis_index("tm")]).astype(jnp.int32)

    occ = columns[:NOCC].reshape(2, own_occ, rows)
    occ_mine = lax.dynamic_index_in_dim(occ, core, 0, keepdims=False)
    occ_theirs = lax.dynamic_index_in_dim(occ, 1 - core, 0, keepdims=False)
    occ_pair = jnp.stack([occ_mine, lax.ppermute(occ_theirs, "space", swap)])
    splits = tm if tm == 2 else 1
    emp_columns = lax.dynamic_slice(
        columns.reshape((NOCC + NEMP) // own_emp, splits, own_emp // splits, rows),
        (NOCC // own_emp, lax.axis_index("tm") % splits, 0, 0),
        (chips, 1, own_emp // splits, rows),
    )
    emp = lax.all_to_all(
        emp_columns.reshape(chips, own_emp // splits, rows),
        "space",
        split_axis=0,
        concat_axis=0,
        axis_index_groups=[[2 * k + c for k in range(chips)] for c in range(2)],
    )

    tables = class_tables(hold(jnp.zeros((1,), jnp.int32), occ_pair))
    emp_parts = []
    ahead, back = ring_steps(chips)
    found, offsets = [occ_pair], [0]
    from_left = from_right = occ_pair
    for hop in range(1, chips // 2 + 1):
        if hop == 2:
            from_left, from_right, emp, tables = lax.optimization_barrier((from_left, from_right, emp, tables))
            traded = lax.ppermute(emp, "tm", [(0, 1), (1, 0)]) if splits > 1 else None
        elif hop == 3:
            from_left, from_right, emp, traded = lax.optimization_barrier((from_left, from_right, emp, traded))
            emp_parts += [emp, lax.ppermute(emp, "space", swap)]
            if splits > 1:
                emp_parts += [traded, lax.ppermute(traded, "space", swap)]
            held_times = hold(times, (from_left, from_right))
            every_time = [times] + [
                lax.ppermute(held_times, "tm", [((d + step) % tm, d) for d in range(tm)]) for step in range(1, tm)
            ]
        elif hop == 4:
            from_left, from_right = lax.optimization_barrier((from_left, from_right))
            scalars = jnp.concatenate([gaps] + every_time + [cos_weights.reshape(-1)])
            weights = all_pair_weights(
                place, hold(scalars, (from_left, from_right)), tm, own_count, time_count, own_occ, own_emp
            )
        elif hop > 4:
            from_left, from_right = lax.optimization_barrier((from_left, from_right))
        from_left = lax.ppermute(from_left, "space", ahead)
        found.append(from_left)
        offsets.append(-hop)
        if 2 * hop < chips:
            from_right = lax.ppermute(from_right, "space", back)
            found.append(from_right)
            offsets.append(hop)

    results = []
    part_rows = NG // space
    for w in range(own_count):
        keep_far, send_far, keep_near, send_near = pair_moment(
            place, weights[w], found, offsets, emp_parts, tables
        )
        far_total = keep_far + lax.ppermute(send_far, "space", swap).astype(jnp.float32)
        near_total = keep_near + lax.ppermute(send_near, "space", swap).astype(jnp.float32)
        far = far_slots(chips)
        near = [slot for slot in range(chips) if slot not in far]
        totals = {}
        for slots, total in ((far, far_total), (near, near_total)):
            for index, slot in enumerate(slots):
                start = index * round_up(part_rows, 16)
                totals[slot] = total[start : start + part_rows]
        results.append(reduce_ring(totals, chips))
    return jnp.stack(results)


def solution(mesh):
    return jax.shard_map(
        functools.partial(local, mesh.shape["space"], mesh.shape["tm"]),
        mesh=mesh,
        in_specs=(P("space", None), P(), P("tm"), P()),
        out_specs=P("tm", "space", None),
        check_vma=False,
    )
```
